512 devices in a mesh: wide: 64 (over z, y_hi, core), narrow: 8 (over y_lo, x).
Axes of the slice: x: 4, y: 8 (y_hi: 4, y_lo: 2; y = y_hi * 2 + y_lo), z: 8, core: 2. Of those that a mesh axis runs over, the one named last changes fastest.
Arguments:
- activations: bfloat16 [32768, 4096], P('wide', 'narrow'), may hold values from -3 to 3
- out_grads: bfloat16 [32768, 1536], P('wide'), may hold values from -8 to 8
- in_basis: bfloat16 [4096, 4096], P('wide', 'narrow'), may hold values from -8 to 8, as said below
- out_basis: bfloat16 [1536, 1536], P('narrow'), may hold values from -8 to 8, as said below
- valid: int32 [32768], P('wide'), may hold values 0 or 1
Outputs:
- corrected: float32 [1536, 4096], P('wide', 'narrow')
The draws below stay inside these ranges and needn't reach their ends.
Inputs may be any that keep to these rules, and one draw needn't show every extreme that they name: in_basis is a square basis with a dominant diagonal. out_basis is a square basis with a dominant diagonal.
All inputs are finite; a program needn't handle non-finite values. No bound on the sum of `valid` on one device may be relied on, other than what follows from the above.
Results may differ from the reference program's by a relative error of at most 0.0012.
Values may be sent and summed in bfloat16 or wider, within the bound.
No kernel may reach another device: no remote copies, remote signals or barrier semaphores. Data moves between devices by JAX's collectives and lax.ppermute only.
A program may use at most 64 MiB of HBM per device.

```python
import jax
import jax.numpy as jnp
from jax import lax

D_IN = 4096
D_OUT = 1536
SEQ = 128
TOKENS = 32768
NSEQ = 256


def basis_draw(key, order):
    noise_key = jax.random.fold_in(key, 0)
    noise = jax.random.normal(noise_key, (order, order), jnp.float32) * (0.5 / order ** 0.5)
    return (jnp.eye(order, dtype=jnp.float32) + noise).astype(jnp.bfloat16)


def draw_in_basis(key, part):
    key = jax.random.fold_in(key, 11)
    return basis_draw(key, D_IN)


def draw_out_basis(key, part):
    key = jax.random.fold_in(key, 23)
    return basis_draw(key, D_OUT)


def plant(drawn, own_key, low, top_value):
    spot = [jax.random.randint(jax.random.fold_in(own_key, axis), (), 0, length) for axis, length in enumerate(drawn.shape)]
    longest = drawn.shape.index(max(drawn.shape))
    next_to = spot[:longest] + [(spot[longest] + 1) % drawn.shape[longest]] + spot[longest + 1:]
    return drawn.at[tuple(spot)].set(low).at[tuple(next_to)].set(top_value)


def with_spikes(result, key, source, target, parts, factor):
    owner, partner = [(jnp.arange(result.shape[dim]) // (result.shape[dim] // parts)).reshape([-1 if axis == dim else 1 for axis in range(result.ndim)]) for dim in (source, target)]
    chosen = jax.random.permutation(key, parts)[partner]
    strong = (owner == chosen) | (owner == (partner + parts // 2) % parts)
    return jnp.where(strong, factor * result, result)


def shard_levels(own_key, dims, cuts, least, largest):
    gain, own = 1.0, jax.random.fold_in(own_key, 6)
    for dim, blocks in cuts:
        heights = jnp.exp(jax.random.uniform(jax.random.fold_in(own, dim), (blocks,), jnp.float32, least / len(cuts), largest / len(cuts)))
        gain = gain * jnp.repeat(heights, dims[dim] // blocks).reshape([-1 if axis == dim else 1 for axis in range(len(dims))])
    return gain


def gaussian(key, extent, width, reach, cuts=(), kind=jnp.bfloat16):
    array = jax.random.normal(key, extent, jnp.float32) * width
    if len(cuts) > 0:
        array = shard_levels(key, extent, cuts, -0.22, 0.18) * array
    return jnp.clip(array, min=-reach, max=reach).astype(kind)


def bell_draw_with(rng, extent, spread, limit, cuts, heavy, kind=jnp.bfloat16):
    entries = spread * jax.random.normal(rng, extent, jnp.float32)
    if cuts:
        entries = entries * shard_levels(rng, extent, cuts, -0.22, 0.18)
    return jnp.clip(with_spikes(entries, jax.random.fold_in(rng, 3), *heavy), -limit, limit).astype(kind)


def setup_inputs(seed: int = 0) -> dict:
    key_list = jax.random.split(jax.random.key(seed), 6)
    return {
        "activations": gaussian(key_list[0], (TOKENS, D_IN), 0.5, 3.0, ((0, 64), (1, 8))),
        "out_grads": bell_draw_with(key_list[1], (TOKENS, D_OUT), 0.5, 8.0, ((0, 64),), (0, 1, 64, 4.0)),
        "in_basis": draw_in_basis(jax.random.fold_in(key_list[5], 71), 0),
        "out_basis": draw_out_basis(jax.random.fold_in(key_list[5], 71), 0),
        "valid": plant((jax.random.randint(key_list[4], (TOKENS,), 0, 16) < 13).astype(jnp.int32), jax.random.fold_in(key_list[4], 1), 0, 1),
    }


def reference(activations, out_grads, in_basis, out_basis, valid):
    rotated_in = jnp.dot(activations, in_basis, preferred_element_type=jnp.float32).astype(jnp.bfloat16)
    rotated_out = jnp.dot(out_grads, out_basis, preferred_element_type=jnp.float32).astype(jnp.bfloat16)
    routed = valid.astype(jnp.bfloat16)
    masked_in = rotated_in * routed[:, None]
    seq_in = masked_in.reshape(NSEQ, SEQ, D_IN)
    seq_out = rotated_out.reshape(NSEQ, SEQ, D_OUT)

    def accumulate(running, pair):
        grads_seq, inputs_seq = pair
        product = lax.dot_general(grads_seq, inputs_seq, (((0,), (0,)), ((), ())), preferred_element_type=jnp.float32)
        return running + product * product, None

    running, _ = lax.scan(accumulate, jnp.zeros((D_OUT, D_IN), jnp.float32), (seq_out, seq_in))
    return running / NSEQ
```

```python
import functools

import jax
import jax.numpy as jnp
import numpy as np
from jax import lax
from jax.experimental import pallas as pl
from jax.experimental.pallas import tpu as pltpu
from jax.sharding import PartitionSpec as P

SEQ = 128
NZ, NYH, NC, NYL, NX = 8, 4, 2, 2, 4
BOTH = ("wide", "narrow")
F32, BF16, F16 = jnp.float32, jnp.bfloat16, jnp.float16
VMEM = pl.BlockSpec(memory_space=pltpu.VMEM)
SMEM = pl.BlockSpec(memory_space=pltpu.SMEM)
LIMIT = 48 * 1024 * 1024


def send(value, target):
    pairs = []
    for z, yh, c, yl, x in np.ndindex(NZ, NYH, NC, NYL, NX):
        z2, yh2, c2, yl2, x2 = target(z, yh, c, yl, x)
        z2, yh2, c2, yl2, x2 = z2 % NZ, yh2 % NYH, c2 % NC, yl2 % NYL, x2 % NX
        source = (((z * NYH + yh) * NC + c) * NYL + yl) * NX + x
        pairs.append((source, (((z2 * NYH + yh2) * NC + c2) * NYL + yl2) * NX + x2))
    return lax.ppermute(value, BOTH, pairs)


def other_core(value):
    return send(value, lambda z, yh, c, yl, x: (z, yh, c + 1, yl, x))


def cost(flops, nbytes):
    return pl.CostEstimate(flops=flops, bytes_accessed=nbytes, transcendentals=0)


def call(kernel, out, scratch, flops, nbytes, n_vmem):
    return pl.pallas_call(
        kernel,
        out_shape=out,
        in_specs=[SMEM] + [VMEM] * n_vmem,
        out_specs=VMEM,
        scratch_shapes=scratch,
        compiler_params=pltpu.CompilerParams(vmem_limit_bytes=LIMIT),
        cost_estimate=cost(flops, nbytes),
    )


def rotate_out_kernel(pos, grads, *refs):
    pieces, out, basis = refs[:NX], refs[NX], refs[NX + 1]
    rows = pieces[0].shape[0] // NYL
    yl, x = pos[1], pos[2]
    for d in range(NX):
        for flip in range(NYL):
            owner = lax.rem(yl + flip, NYL) * NX + lax.rem(x - d + NX, NX)
            at = pl.multiple_of(owner * rows, 64)
            basis[pl.ds(at, rows), :] = pieces[d][flip * rows : (flip + 1) * rows, :]
    width = 256
    for j in range(out.shape[1] // width):
        cols = slice(j * width, (j + 1) * width)
        out[:, cols] = jnp.dot(grads[...], basis[:, cols], preferred_element_type=F32).astype(out.dtype)


def rotate_out(pos, grads, pieces):
    tokens, depth = grads.shape
    width = pieces[0].shape[1]
    return call(
        rotate_out_kernel,
        jax.ShapeDtypeStruct((tokens, width), BF16),
        [pltpu.VMEM((depth, width), BF16)],
        2 * tokens * depth * width,
        2 * (tokens * depth + depth * width + tokens * width),
        1 + NX,
    )(pos, grads, *pieces)


def rotate_in_kernel(pos, acts, mask, mine, other, out):
    z, core = pos[0], pos[3]
    chunk = mine.shape[0] // NZ
    half = out.shape[0] // 2
    for part in range(2):
        rows = slice(part * half, (part + 1) * half)
        total = jnp.zeros((half, out.shape[1]), F32)
        for r in range(NZ):
            plane = lax.rem(z - r + NZ, NZ) * (2 * chunk)
            for ref, c in ((mine, core), (other, 1 - core)):
                at = pl.multiple_of(plane + c * chunk, chunk)
                total += jnp.dot(
                    acts[rows, pl.ds(at, chunk)],
                    ref[r * chunk : (r + 1) * chunk, :],
                    preferred_element_type=F32,
                )
        kept = total.astype(BF16).astype(F32) * mask[rows, :]
        out[rows, :] = kept.astype(BF16)


def rotate_in(pos, acts, mask, mine, other):
    tokens, depth = acts.shape
    width = mine.shape[1]
    return call(
        rotate_in_kernel,
        jax.ShapeDtypeStruct((tokens, width), BF16),
        [],
        2 * tokens * depth * width,
        2 * (tokens * depth + depth * width + tokens * width),
        4,
    )(pos, acts, mask, mine, other)


def squares_kernel(pos, outs, ins, out):
    width = 256
    for j in range(out.shape[0] // width):
        cols = slice(j * width, (j + 1) * width)
        total = None
        for s in range(outs.shape[0] // SEQ):
            rows = slice(s * SEQ, (s + 1) * SEQ)
            grad = lax.dot_general(
                outs[rows, cols], ins[rows, :], (((0,), (0,)), ((), ())), preferred_element_type=F32
            )
            total = grad * grad if total is None else total + grad * grad
        out[cols, :] = total


def squares(pos, outs, ins):
    tokens, width = outs.shape
    return call(
        squares_kernel,
        jax.ShapeDtypeStruct((width, ins.shape[1]), F32),
        [],
        2 * tokens * width * ins.shape[1],
        2 * tokens * (width + ins.shape[1]) + 4 * width * ins.shape[1],
        2,
    )(pos, outs, ins)


def gather_in_basis(in_basis, z, yh):
    rows = in_basis.shape[0]

    def to(j):
        def target(z, yh, c, yl, x):
            i = (yh % 2) * 2 + c
            return z, i - j, yh // 2, yl, x

        return target

    got = [send(in_basis, to(j)) for j in range(NYH)]
    chunk = lax.dynamic_slice_in_dim(
        jnp.concatenate(got + got, axis=0), lax.rem(NYH - yh, NYH) * rows, NYH * rows, 0
    )
    up = lambda z, yh, c, yl, x: (z + 1, yh, c, yl, x)
    down = lambda z, yh, c, yl, x: (z - 1, yh, c, yl, x)
    from_below, from_above = [chunk], [chunk]
    for _ in range(3):
        from_below.append(send(from_below[-1], up))
        from_above.append(send(from_above[-1], down))
    half = chunk.shape[0] // 2
    far = [send(from_below[-1][:half], up), send(from_above[-1][half:], down)]
    return jnp.concatenate(from_below + far + from_above[:0:-1], axis=0)


def gather_out_basis(out_basis, core):
    width = out_basis.shape[1]
    own = width // (NZ * NYH * NC)
    source = lax.broadcasted_iota(jnp.int32, (width, width // NC), 0)
    place = lax.broadcasted_iota(jnp.int32, (width, width // NC), 1)
    wanted = ((place // own) * NC + core) * own + place % own
    picked = jnp.dot(out_basis, (source == wanted).astype(BF16), preferred_element_type=F32).astype(BF16)
    pair = jnp.concatenate([picked, send(picked, lambda z, yh, c, yl, x: (z, yh, c, yl + 1, x))], axis=0)
    pieces = [pair]
    for d in range(1, NX):
        pieces.append(send(pair, functools.partial(lambda d, z, yh, c, yl, x: (z, yh, c, yl, x + d), d)))
    return pieces


def scatter_sum(total):
    blocks = NZ * NYH
    groups = [[zy * NC + c for zy in range(blocks)] for c in range(NC)]
    rows, columns = total.shape[0] // blocks, total.shape[1]
    tiles = (rows // 8, columns // 128)
    top = jnp.max(total)
    power = jnp.maximum(jnp.floor(jnp.log2(jnp.maximum(top, 1e-30))), -100.0)
    coded = (total * jnp.exp2(14.0 - power)).astype(F16)
    coded = coded.reshape(blocks, tiles[0], 8, tiles[1], 128).transpose(0, 1, 3, 2, 4).reshape(blocks, -1, 128)
    label = jnp.broadcast_to(power.astype(F16), (blocks, 8, 128))
    got = lax.all_to_all(
        jnp.concatenate([coded, label], axis=1), "wide", 0, 0, tiled=True, axis_index_groups=groups
    )
    scale = jnp.exp2(got[:, -8:-7, :1].astype(F32) - 14.0)
    summed = jnp.sum(got[:, :-8, :].astype(F32) * scale, axis=0)
    return summed.reshape(tiles[0], tiles[1], 8, 128).transpose(0, 2, 1, 3).reshape(rows, columns)


def shards(activations, out_grads, in_basis, out_basis, valid):
    wide, narrow = lax.axis_index("wide"), lax.axis_index("narrow")
    z, yh, core = wide // (NYH * NC), (wide // NC) % NYH, wide % NC
    yl, x = narrow // NX, narrow % NX
    pos = jnp.stack([z, yl, x, core]).astype(jnp.int32)
    sequences = activations.shape[0] // SEQ * lax.axis_size("wide")

    acts = lax.all_gather(activations, "narrow", axis=1, tiled=True)
    mine = gather_in_basis(in_basis, z, yh)
    other = other_core(mine)
    pieces = gather_out_basis(out_basis, core)
    pieces_other = [other_core(piece) for piece in [jnp.concatenate(pieces, axis=0)]][0]
    pieces_other = jnp.split(pieces_other, NX, axis=0)

    mask = valid.astype(F32)[:, None]
    masked_in = rotate_in(pos, acts, mask, mine, other)
    out_other = rotate_out(pos, out_grads, pieces_other)
    out_mine = rotate_out(pos, out_grads, pieces)
    total = other_core(squares(pos, out_other, masked_in)) + squares(pos, out_mine, masked_in)
    return scatter_sum(total) / sequences


def solution(mesh):
    in_specs = (
        P("wide", "narrow"),
        P("wide", None),
        P("wide", "narrow"),
        P("narrow", None),
        P("wide"),
    )
    out_specs = P("wide", "narrow")
    return jax.shard_map(shards, mesh=mesh, in_specs=in_specs, out_specs=out_specs, check_vma=False)
```

```python
import functools

import jax
import jax.numpy as jnp
import numpy as np
from jax import lax
from jax.experimental import pallas as pl
from jax.experimental.pallas import tpu as pltpu
from jax.sharding import PartitionSpec as P

SEQ = 128
NZ, NYH, NC, NYL, NX = 8, 4, 2, 2, 4
BOTH = ("wide", "narrow")
F32, BF16, F16 = jnp.float32, jnp.bfloat16, jnp.float16
VMEM = pl.BlockSpec(memory_space=pltpu.VMEM)
SMEM = pl.BlockSpec(memory_space=pltpu.SMEM)
LIMIT = 48 * 1024 * 1024


def send(value, target):
    pairs = []
    for z, yh, c, yl, x in np.ndindex(NZ, NYH, NC, NYL, NX):
        z2, yh2, c2, yl2, x2 = target(z, yh, c, yl, x)
        z2, yh2, c2, yl2, x2 = z2 % NZ, yh2 % NYH, c2 % NC, yl2 % NYL, x2 % NX
        source = (((z * NYH + yh) * NC + c) * NYL + yl) * NX + x
        pairs.append((source, (((z2 * NYH + yh2) * NC + c2) * NYL + yl2) * NX + x2))
    return lax.ppermute(value, BOTH, pairs)


def other_core(value):
    return send(value, lambda z, yh, c, yl, x: (z, yh, c + 1, yl, x))


def cost(flops, nbytes):
    return pl.CostEstimate(flops=flops, bytes_accessed=nbytes, transcendentals=0)


def call(kernel, out, scratch, flops, nbytes, n_vmem):
    return pl.pallas_call(
        kernel,
        out_shape=out,
        in_specs=[SMEM] + [VMEM] * n_vmem,
        out_specs=VMEM,
        scratch_shapes=scratch,
        compiler_params=pltpu.CompilerParams(vmem_limit_bytes=LIMIT),
        cost_estimate=cost(flops, nbytes),
    )


def rotate_out_kernel(pos, grads, *refs):
    pieces, out, basis = refs[:NX], refs[NX], refs[NX + 1]
    rows = pieces[0].shape[0] // NYL
    yl, x = pos[1], pos[2]
    for d in range(NX):
        for flip in range(NYL):
            owner = lax.rem(yl + flip, NYL) * NX + lax.rem(x - d + NX, NX)
            at = pl.multiple_of(owner * rows, 64)
            basis[pl.ds(at, rows), :] = pieces[d][flip * rows : (flip + 1) * rows, :]
    width = 256
    for j in range(out.shape[1] // width):
        cols = slice(j * width, (j + 1) * width)
        out[:, cols] = jnp.dot(grads[...], basis[:, cols], preferred_element_type=F32).astype(out.dtype)


def rotate_out(pos, grads, pieces):
    tokens, depth = grads.shape
    width = pieces[0].shape[1]
    return call(
        rotate_out_kernel,
        jax.ShapeDtypeStruct((tokens, width), BF16),
        [pltpu.VMEM((depth, width), BF16)],
        2 * tokens * depth * width,
        2 * (tokens * depth + depth * width + tokens * width),
        1 + NX,
    )(pos, grads, *pieces)


def arrange_kernel(pos, *refs):
    pieces, out = refs[:NX], refs[NX]
    x = pos[2]
    half = out.shape[2] // NX
    for d in range(NX):
        at = pl.multiple_of(lax.rem(x - d + NX, NX) * half, half)
        for c in range(NC):
            out[c, :, pl.ds(at, half)] = pieces[d][:, c * half : (c + 1) * half]


def arrange(pos, pieces):
    tokens, width = pieces[0].shape
    return call(
        arrange_kernel,
        jax.ShapeDtypeStruct((NC, tokens, NX * width // NC), BF16),
        [],
        0,
        4 * tokens * NX * width,
        NX,
    )(pos, *pieces)


def partial_kernel(flip, pos, acts, mine, other, out):
    core = pos[3]
    depth = acts.shape[2]
    rows = pl.ds(pl.multiple_of(lax.rem(pos[1] + flip, NYL) * depth, depth), depth)
    width = 256
    for j in range(out.shape[1] // width):
        cols = slice(j * width, (j + 1) * width)
        out[:, cols] = jnp.dot(acts[core], mine[rows, cols], preferred_element_type=F32) + jnp.dot(
            acts[1 - core], other[rows, cols], preferred_element_type=F32
        )


def partial(flip, pos, acts, mine, other):
    tokens, depth = acts.shape[1], NC * acts.shape[2]
    width = mine.shape[1]
    return call(
        functools.partial(partial_kernel, flip),
        jax.ShapeDtypeStruct((tokens, width), F32),
        [],
        2 * tokens * depth * width,
        2 * (tokens * depth + depth * width) + 4 * tokens * width,
        3,
    )(pos, acts, mine, other)


def squares_kernel(pos, outs, ins, out):
    width = 256
    for j in range(out.shape[0] // width):
        cols = slice(j * width, (j + 1) * width)
        total = None
        for s in range(outs.shape[0] // SEQ):
            rows = slice(s * SEQ, (s + 1) * SEQ)
            grad = lax.dot_general(
                outs[rows, cols], ins[rows, :], (((0,), (0,)), ((), ())), preferred_element_type=F32
            )
            total = grad * grad if total is None else total + grad * grad
        out[cols, :] = total


def squares(pos, outs, ins):
    tokens, width = outs.shape
    return call(
        squares_kernel,
        jax.ShapeDtypeStruct((width, ins.shape[1]), F32),
        [],
        2 * tokens * width * ins.shape[1],
        2 * tokens * (width + ins.shape[1]) + 4 * width * ins.shape[1],
        2,
    )(pos, outs, ins)


def place_in_basis(in_basis, yh):
    rows = in_basis.shape[0]

    def to(j):
        def target(z, yh, c, yl, x):
            i = (yh % 2) * 2 + c
            return yl * (NZ // 2) + z % (NZ // 2), i - j, yh // 2, z // (NZ // 2), x

        return target

    got = [send(in_basis, to(j)) for j in range(NYH)]
    return lax.dynamic_slice_in_dim(
        jnp.concatenate(got + got, axis=0), lax.rem(NYH - yh, NYH) * rows, NYH * rows, 0
    )


def gather_in_basis(chunk):
    groups = [[z * NYH * NC + r for z in range(NZ)] for r in range(NYH * NC)]
    return lax.all_gather(chunk, "wide", axis=0, tiled=True, axis_index_groups=groups)


def along_x(value):
    pieces = [value]
    for d in range(1, NX):
        pieces.append(send(value, functools.partial(lambda d, z, yh, c, yl, x: (z, yh, c, yl, x + d), d)))
    return pieces


def power_of(top):
    return jnp.maximum(jnp.floor(jnp.log2(jnp.maximum(top, 1e-30))), -100.0)


def swap_partial(value):
    power = power_of(jnp.max(jnp.abs(value)))
    coded = (value * jnp.exp2(14.0 - power)).astype(F16)
    label = jnp.broadcast_to(power.astype(F16), (8, value.shape[1]))
    got = send(jnp.concatenate([coded, label], axis=0), lambda z, yh, c, yl, x: (z, yh, c, yl + 1, x))
    return got[:-8].astype(F32) * jnp.exp2(got[-8:-7, :1].astype(F32) - 14.0)


def pair_out_basis(out_basis, core):
    width = out_basis.shape[1]
    own = width // (NZ * NYH * NC)
    source = lax.broadcasted_iota(jnp.int32, (width, width // NC), 0)
    place = lax.broadcasted_iota(jnp.int32, (width, width // NC), 1)
    wanted = ((place // own) * NC + core) * own + place % own
    picked = jnp.dot(out_basis, (source == wanted).astype(BF16), preferred_element_type=F32).astype(BF16)
    return jnp.concatenate([picked, send(picked, lambda z, yh, c, yl, x: (z, yh, c, yl + 1, x))], axis=0)


def scatter_sum(total):
    blocks = NZ * NYH
    groups = [[zy * NC + c for zy in range(blocks)] for c in range(NC)]
    rows, columns = total.shape[0] // blocks, total.shape[1]
    tiles = (rows // 8, columns // 128)
    power = power_of(jnp.max(total))
    coded = (total * jnp.exp2(14.0 - power)).astype(F16)
    coded = coded.reshape(blocks, tiles[0], 8, tiles[1], 128).transpose(0, 1, 3, 2, 4).reshape(blocks, -1, 128)
    label = jnp.broadcast_to(power.astype(F16), (blocks, 8, 128))
    got = lax.all_to_all(
        jnp.concatenate([coded, label], axis=1), "wide", 0, 0, tiled=True, axis_index_groups=groups
    )
    scale = jnp.exp2(got[:, -8:-7, :1].astype(F32) - 14.0)
    summed = jnp.sum(got[:, :-8, :].astype(F32) * scale, axis=0)
    return summed.reshape(tiles[0], tiles[1], 8, 128).transpose(0, 2, 1, 3).reshape(rows, columns)


def shards(activations, out_grads, in_basis, out_basis, valid):
    wide, narrow = lax.axis_index("wide"), lax.axis_index("narrow")
    z, yh, core = wide // (NYH * NC), (wide // NC) % NYH, wide % NC
    yl, x = narrow // NX, narrow % NX
    pos = jnp.stack([z, yl, x, core]).astype(jnp.int32)
    sequences = activations.shape[0] // SEQ * lax.axis_size("wide")

    chunk = place_in_basis(in_basis, yh)
    pair = pair_out_basis(out_basis, core)
    activations, chunk, pair = lax.optimization_barrier((activations, chunk, pair))
    mine = gather_in_basis(chunk)
    acts_pieces = along_x(activations)
    *acts_pieces, pair = lax.optimization_barrier((*acts_pieces, pair))
    acts = arrange(pos, acts_pieces)
    pieces = along_x(pair)
    mine, *pieces = lax.optimization_barrier((mine, *pieces))
    other = other_core(mine)
    pieces_other = jnp.split(other_core(jnp.concatenate(pieces, axis=0)), NX, axis=0)

    theirs = swap_partial(partial(1, pos, acts, mine, other))
    rotated_in = (partial(0, pos, acts, mine, other) + theirs).astype(BF16)
    masked_in = rotated_in * valid.astype(BF16)[:, None]
    out_other = rotate_out(pos, out_grads, pieces_other)
    out_mine = rotate_out(pos, out_grads, pieces)
    total = other_core(squares(pos, out_other, masked_in)) + squares(pos, out_mine, masked_in)
    return scatter_sum(total) / sequences


def solution(mesh):
    in_specs = (
        P("wide", "narrow"),
        P("wide", None),
        P("wide", "narrow"),
        P("narrow", None),
        P("wide"),
    )
    out_specs = P("wide", "narrow")
    return jax.shard_map(shards, mesh=mesh, in_specs=in_specs, out_specs=out_specs, check_vma=False)
```

```python
import functools

import jax
import jax.numpy as jnp
import numpy as np
from jax import lax
from jax.experimental import pallas as pl
from jax.experimental.pallas import tpu as pltpu
from jax.sharding import PartitionSpec as P

SEQ = 128
NZ, NYH, NC, NYL, NX = 8, 4, 2, 2, 4
BOTH = ("wide", "narrow")
F32, BF16, F16 = jnp.float32, jnp.bfloat16, jnp.float16
VMEM = pl.BlockSpec(memory_space=pltpu.VMEM)
SMEM = pl.BlockSpec(memory_space=pltpu.SMEM)
LIMIT = 48 * 1024 * 1024


def send(value, target):
    pairs = []
    for z, yh, c, yl, x in np.ndindex(NZ, NYH, NC, NYL, NX):
        z2, yh2, c2, yl2, x2 = target(z, yh, c, yl, x)
        z2, yh2, c2, yl2, x2 = z2 % NZ, yh2 % NYH, c2 % NC, yl2 % NYL, x2 % NX
        source = (((z * NYH + yh) * NC + c) * NYL + yl) * NX + x
        pairs.append((source, (((z2 * NYH + yh2) * NC + c2) * NYL + yl2) * NX + x2))
    return lax.ppermute(value, BOTH, pairs)


def other_core(value):
    return send(value, lambda z, yh, c, yl, x: (z, yh, c + 1, yl, x))


def cost(flops, nbytes):
    return pl.CostEstimate(flops=flops, bytes_accessed=nbytes, transcendentals=0)


def call(kernel, out, scratch, flops, nbytes, n_vmem):
    return pl.pallas_call(
        kernel,
        out_shape=out,
        in_specs=[SMEM] + [VMEM] * n_vmem,
        out_specs=VMEM,
        scratch_shapes=scratch,
        compiler_params=pltpu.CompilerParams(vmem_limit_bytes=LIMIT),
        cost_estimate=cost(flops, nbytes),
    )


def rotate_out_kernel(pos, grads, own, flipped, out, basis):
    rows = own.shape[0] // NX
    for ref, yl in ((own, pos[1]), (flipped, 1 - pos[1])):
        for d in range(NX):
            at = pl.multiple_of((yl * NX + lax.rem(pos[2] - d + NX, NX)) * rows, 64)
            basis[pl.ds(at, rows), :] = ref[d * rows : (d + 1) * rows, :]
    width = 256
    for j in range(out.shape[1] // width):
        cols = slice(j * width, (j + 1) * width)
        out[:, cols] = jnp.dot(grads[...], basis[:, cols], preferred_element_type=F32).astype(out.dtype)


def rotate_out(pos, grads, own, flipped):
    tokens, depth = grads.shape
    width = own.shape[1]
    return call(
        rotate_out_kernel,
        jax.ShapeDtypeStruct((tokens, width), BF16),
        [pltpu.VMEM((depth, width), BF16)],
        2 * tokens * depth * width,
        2 * (tokens * depth + depth * width + tokens * width),
        3,
    )(pos, grads, own, flipped)


def arrange_kernel(pos, acts, out):
    half = acts.shape[1] // (NZ * NC)
    for z in range(NZ):
        for c in range(NC):
            at = (z * NC + c) * half
            out[c, :, z * half : (z + 1) * half] = acts[:, at : at + half]


def arrange(pos, acts):
    tokens, depth = acts.shape
    return call(
        arrange_kernel,
        jax.ShapeDtypeStruct((NC, tokens, depth // NC), BF16),
        [],
        0,
        4 * tokens * depth,
        1,
    )(pos, acts)


def first_half_kernel(pos, acts, mine, out):
    core, width = pos[3], 256
    for j in range(out.shape[1] // width):
        cols = slice(j * width, (j + 1) * width)
        out[:, cols] = jnp.dot(acts[core], mine[:, cols], preferred_element_type=F32)


def first_half(pos, acts, mine):
    _, tokens, depth = acts.shape
    width = mine.shape[1]
    return call(
        first_half_kernel,
        jax.ShapeDtypeStruct((tokens, width), F32),
        [],
        2 * tokens * depth * width,
        2 * (tokens * depth + depth * width) + 4 * tokens * width,
        2,
    )(pos, acts, mine)


def masked_kernel(pos, acts, other, first, mask, out):
    core, width = pos[3], 256
    for j in range(out.shape[1] // width):
        cols = slice(j * width, (j + 1) * width)
        total = first[:, cols] + jnp.dot(acts[1 - core], other[:, cols], preferred_element_type=F32)
        out[:, cols] = (total.astype(BF16).astype(F32) * mask[...]).astype(BF16)


def masked(pos, acts, other, first, mask):
    _, tokens, depth = acts.shape
    width = other.shape[1]
    return call(
        masked_kernel,
        jax.ShapeDtypeStruct((tokens, width), BF16),
        [],
        2 * tokens * depth * width,
        2 * (tokens * depth + depth * width) + 6 * tokens * width,
        4,
    )(pos, acts, other, first, mask)


def squares_kernel(pos, outs, ins, out):
    width = 256
    for j in range(out.shape[0] // width):
        cols = slice(j * width, (j + 1) * width)
        total = None
        for s in range(outs.shape[0] // SEQ):
            rows = slice(s * SEQ, (s + 1) * SEQ)
            grad = lax.dot_general(
                outs[rows, cols], ins[rows, :], (((0,), (0,)), ((), ())), preferred_element_type=F32
            )
            total = grad * grad if total is None else total + grad * grad
        out[cols, :] = total


def squares(pos, outs, ins):
    tokens, width = outs.shape
    return call(
        squares_kernel,
        jax.ShapeDtypeStruct((width, ins.shape[1]), F32),
        [],
        2 * tokens * width * ins.shape[1],
        2 * tokens * (width + ins.shape[1]) + 4 * width * ins.shape[1],
        2,
    )(pos, outs, ins)


def place_in_basis(in_basis, yh):
    rows = in_basis.shape[0]

    def to(j):
        def target(z, yh, c, yl, x):
            i = (yh % 2) * 2 + c
            return z, i - j, yh // 2, yl, x

        return target

    got = [send(in_basis, to(j)) for j in range(NYH)]
    return lax.dynamic_slice_in_dim(
        jnp.concatenate(got + got, axis=0), lax.rem(NYH - yh, NYH) * rows, NYH * rows, 0
    )


def gather_in_basis(chunk):
    groups = [[z * NYH * NC + r for z in range(NZ)] for r in range(NYH * NC)]
    copies = jnp.concatenate([chunk] * NZ, axis=0)
    return lax.all_to_all(copies, "wide", 0, 0, tiled=True, axis_index_groups=groups)


def from_x(value):
    pieces = [value]
    for d in range(1, NX):
        pieces.append(send(value, functools.partial(lambda d, z, yh, c, yl, x: (z, yh, c, yl, x + d), d)))
    return pieces


def other_yl(value):
    half = value.shape[0] // 2
    up = lambda z, yh, c, yl, x: (z, yh + yl, c, yl + 1, x)
    down = lambda z, yh, c, yl, x: (z, yh + yl - 1, c, yl + 1, x)
    return jnp.concatenate([send(value[:half], up), send(value[half:], down)], axis=0)


def power_of(top):
    return jnp.maximum(jnp.floor(jnp.log2(jnp.maximum(top, 1e-30))), -100.0)


def pick(out_basis, core):
    width = out_basis.shape[1]
    own = width // (NZ * NYH * NC)
    source = lax.broadcasted_iota(jnp.int32, (width, width // NC), 0)
    place = lax.broadcasted_iota(jnp.int32, (width, width // NC), 1)
    wanted = ((place // own) * NC + core) * own + place % own
    return jnp.dot(out_basis, (source == wanted).astype(BF16), preferred_element_type=F32).astype(BF16)


def scatter_sum(total):
    blocks = NZ * NYH
    groups = [[zy * NC + c for zy in range(blocks)] for c in range(NC)]
    rows, columns = total.shape[0] // blocks, total.shape[1]
    tiles = (rows // 8, columns // 128)
    power = power_of(jnp.max(total))
    coded = (total * jnp.exp2(14.0 - power)).astype(F16)
    coded = coded.reshape(blocks, tiles[0], 8, tiles[1], 128).transpose(0, 1, 3, 2, 4).reshape(blocks, -1, 128)
    label = jnp.broadcast_to(power.astype(F16), (blocks, 8, 128))
    got = lax.all_to_all(
        jnp.concatenate([coded, label], axis=1), "wide", 0, 0, tiled=True, axis_index_groups=groups
    )
    scale = jnp.exp2(got[:, -8:-7, :1].astype(F32) - 14.0)
    summed = jnp.sum(got[:, :-8, :].astype(F32) * scale, axis=0)
    return summed.reshape(tiles[0], tiles[1], 8, 128).transpose(0, 2, 1, 3).reshape(rows, columns)


def shards(activations, out_grads, in_basis, out_basis, valid):
    wide, narrow = lax.axis_index("wide"), lax.axis_index("narrow")
    z, yh, core = wide // (NYH * NC), (wide // NC) % NYH, wide % NC
    yl, x = narrow // NX, narrow % NX
    pos = jnp.stack([z, yl, x, core]).astype(jnp.int32)
    sequences = activations.shape[0] // SEQ * lax.axis_size("wide")

    acts = lax.all_gather(activations, "narrow", axis=1, tiled=True)
    chunk = place_in_basis(in_basis, yh)
    mine = gather_in_basis(chunk)
    picked, _ = lax.optimization_barrier((pick(out_basis, core), chunk))
    basis_own = jnp.concatenate(from_x(picked), axis=0)
    basis_flipped = other_yl(basis_own)
    basis = jnp.concatenate([basis_own, basis_flipped], axis=0)
    basis_other = other_core(basis)
    half = basis.shape[0] // 2
    out_mine = rotate_out(pos, out_grads, basis_own, basis_flipped)
    out_other = rotate_out(pos, out_grads, basis_other[:half], basis_other[half:])
    acts = arrange(pos, acts)
    mask = valid.astype(F32)[:, None]
    mine, acts, mask, out_mine, out_other = lax.optimization_barrier((mine, acts, mask, out_mine, out_other))
    other = other_core(mine)
    masked_in = masked(pos, acts, other, first_half(pos, acts, mine), mask)
    total = other_core(squares(pos, out_other, masked_in)) + squares(pos, out_mine, masked_in)
    return scatter_sum(total) / sequences


def solution(mesh):
    in_specs = (
        P("wide", "narrow"),
        P("wide", None),
        P("wide", "narrow"),
        P("narrow", None),
        P("wide"),
    )
    out_specs = P("wide", "narrow")
    return jax.shard_map(shards, mesh=mesh, in_specs=in_specs, out_specs=out_specs, check_vma=False)
```

```python
import functools

import jax
import jax.numpy as jnp
import numpy as np
from jax import lax
from jax.experimental import pallas as pl
from jax.experimental.pallas import tpu as pltpu
from jax.sharding import PartitionSpec as P

SEQ = 128
NZ, NYH, NC, NYL, NX = 8, 4, 2, 2, 4
BOTH = ("wide", "narrow")
F32, BF16, F16 = jnp.float32, jnp.bfloat16, jnp.float16
VMEM = pl.BlockSpec(memory_space=pltpu.VMEM)
SMEM = pl.BlockSpec(memory_space=pltpu.SMEM)
LIMIT = 48 * 1024 * 1024


def send(value, target):
    pairs = []
    for z, yh, c, yl, x in np.ndindex(NZ, NYH, NC, NYL, NX):
        z2, yh2, c2, yl2, x2 = target(z, yh, c, yl, x)
        z2, yh2, c2, yl2, x2 = z2 % NZ, yh2 % NYH, c2 % NC, yl2 % NYL, x2 % NX
        source = (((z * NYH + yh) * NC + c) * NYL + yl) * NX + x
        pairs.append((source, (((z2 * NYH + yh2) * NC + c2) * NYL + yl2) * NX + x2))
    return lax.ppermute(value, BOTH, pairs)


def other_core(value):
    return send(value, lambda z, yh, c, yl, x: (z, yh, c + 1, yl, x))


def cost(flops, nbytes):
    return pl.CostEstimate(flops=flops, bytes_accessed=nbytes, transcendentals=0)


def call(kernel, out, scratch, flops, nbytes, n_vmem):
    return pl.pallas_call(
        kernel,
        out_shape=out,
        in_specs=[SMEM] + [VMEM] * n_vmem,
        out_specs=VMEM,
        scratch_shapes=scratch,
        compiler_params=pltpu.CompilerParams(vmem_limit_bytes=LIMIT),
        cost_estimate=cost(flops, nbytes),
    )


def rotate_out_kernel(pos, grads, own, flipped, out, basis):
    rows = own.shape[0] // NX
    for ref, yl in ((own, pos[1]), (flipped, 1 - pos[1])):
        for d in range(NX):
            at = pl.multiple_of((yl * NX + lax.rem(pos[2] - d + NX, NX)) * rows, 64)
            basis[pl.ds(at, rows), :] = ref[d * rows : (d + 1) * rows, :]
    width = 256
    for j in range(out.shape[1] // width):
        cols = slice(j * width, (j + 1) * width)
        out[:, cols] = jnp.dot(grads[...], basis[:, cols], preferred_element_type=F32).astype(out.dtype)


def rotate_out(pos, grads, own, flipped):
    tokens, depth = grads.shape
    width = own.shape[1]
    return call(
        rotate_out_kernel,
        jax.ShapeDtypeStruct((tokens, width), BF16),
        [pltpu.VMEM((depth, width), BF16)],
        2 * tokens * depth * width,
        2 * (tokens * depth + depth * width + tokens * width),
        3,
    )(pos, grads, own, flipped)


def arrange_kernel(pos, *refs):
    pieces, out = refs[:NX], refs[NX]
    x = pos[2]
    half = out.shape[2] // NX
    for d in range(NX):
        at = pl.multiple_of(lax.rem(x - d + NX, NX) * half, half)
        for c in range(NC):
            out[c, :, pl.ds(at, half)] = pieces[d][:, c * half : (c + 1) * half]


def arrange(pos, pieces):
    tokens, width = pieces[0].shape
    return call(
        arrange_kernel,
        jax.ShapeDtypeStruct((NC, tokens, NX * width // NC), BF16),
        [],
        0,
        4 * tokens * NX * width,
        NX,
    )(pos, *pieces)


def partial_kernel(flip, start, pos, acts, mine, other, out):
    core = pos[3]
    depth = acts.shape[2]
    rows = pl.ds(pl.multiple_of(lax.rem(pos[1] + flip, NYL) * depth, depth), depth)
    width = 256
    for j in range(out.shape[1] // width):
        here = slice(j * width, (j + 1) * width)
        cols = slice(start + j * width, start + (j + 1) * width)
        out[:, here] = jnp.dot(acts[core], mine[rows, cols], preferred_element_type=F32) + jnp.dot(
            acts[1 - core], other[rows, cols], preferred_element_type=F32
        )


def partial(flip, start, width, pos, acts, mine, other):
    tokens, depth = acts.shape[1], NC * acts.shape[2]
    return call(
        functools.partial(partial_kernel, flip, start),
        jax.ShapeDtypeStruct((tokens, width), F32),
        [],
        2 * tokens * depth * width,
        2 * (tokens * depth + depth * width) + 4 * tokens * width,
        3,
    )(pos, acts, mine, other)


def squares_kernel(pos, outs, ins, out):
    width = 256
    for j in range(out.shape[0] // width):
        cols = slice(j * width, (j + 1) * width)
        total = None
        for s in range(outs.shape[0] // SEQ):
            rows = slice(s * SEQ, (s + 1) * SEQ)
            grad = lax.dot_general(
                outs[rows, cols], ins[rows, :], (((0,), (0,)), ((), ())), preferred_element_type=F32
            )
            total = grad * grad if total is None else total + grad * grad
        out[cols, :] = total


def squares(pos, outs, ins):
    tokens, width = outs.shape
    return call(
        squares_kernel,
        jax.ShapeDtypeStruct((width, ins.shape[1]), F32),
        [],
        2 * tokens * width * ins.shape[1],
        2 * tokens * (width + ins.shape[1]) + 4 * width * ins.shape[1],
        2,
    )(pos, outs, ins)


def place_in_basis(in_basis, yh):
    rows = in_basis.shape[0]

    def to(j):
        def target(z, yh, c, yl, x):
            i = (yh % 2) * 2 + c
            return yl * (NZ // 2) + z % (NZ // 2), i - j, yh // 2, z // (NZ // 2), x

        return target

    got = [send(in_basis, to(j)) for j in range(NYH)]
    return lax.dynamic_slice_in_dim(
        jnp.concatenate(got + got, axis=0), lax.rem(NYH - yh, NYH) * rows, NYH * rows, 0
    )


def gather_in_basis(chunk):
    groups = [[z * NYH * NC + r for z in range(NZ)] for r in range(NYH * NC)]
    return lax.all_gather(chunk, "wide", axis=0, tiled=True, axis_index_groups=groups)


def from_x(value):
    pieces = [value]
    for d in range(1, NX):
        pieces.append(send(value, functools.partial(lambda d, z, yh, c, yl, x: (z, yh, c, yl, x + d), d)))
    return pieces


def flip_yl(value):
    return send(value, lambda z, yh, c, yl, x: (z, yh, c, yl + 1, x))


def other_yl(value):
    half = value.shape[0] // 2
    up = lambda z, yh, c, yl, x: (z, yh + yl, c, yl + 1, x)
    down = lambda z, yh, c, yl, x: (z, yh + yl - 1, c, yl + 1, x)
    return jnp.concatenate([send(value[:half], up), send(value[half:], down)], axis=0)


def power_of(top):
    return jnp.maximum(jnp.floor(jnp.log2(jnp.maximum(top, 1e-30))), -100.0)


def pick(out_basis, core):
    width = out_basis.shape[1]
    own = width // (NZ * NYH * NC)
    source = lax.broadcasted_iota(jnp.int32, (width, width // NC), 0)
    place = lax.broadcasted_iota(jnp.int32, (width, width // NC), 1)
    wanted = ((place // own) * NC + core) * own + place % own
    return jnp.dot(out_basis, (source == wanted).astype(BF16), preferred_element_type=F32).astype(BF16)


def scatter_sum(total):
    blocks = NZ * NYH
    groups = [[zy * NC + c for zy in range(blocks)] for c in range(NC)]
    rows, columns = total.shape[0] // blocks, total.shape[1]
    tiles = (rows // 8, columns // 128)
    power = power_of(jnp.max(total))
    coded = (total * jnp.exp2(14.0 - power)).astype(F16)
    coded = coded.reshape(blocks, tiles[0], 8, tiles[1], 128).transpose(0, 1, 3, 2, 4).reshape(blocks, -1, 128)
    label = jnp.broadcast_to(power.astype(F16), (blocks, 8, 128))
    got = lax.all_to_all(
        jnp.concatenate([coded, label], axis=1), "wide", 0, 0, tiled=True, axis_index_groups=groups
    )
    scale = jnp.exp2(got[:, -8:-7, :1].astype(F32) - 14.0)
    summed = jnp.sum(got[:, :-8, :].astype(F32) * scale, axis=0)
    return summed.reshape(tiles[0], tiles[1], 8, 128).transpose(0, 2, 1, 3).reshape(rows, columns)


def shards(activations, out_grads, in_basis, out_basis, valid):
    wide, narrow = lax.axis_index("wide"), lax.axis_index("narrow")
    z, yh, core = wide // (NYH * NC), (wide // NC) % NYH, wide % NC
    yl, x = narrow // NX, narrow % NX
    pos = jnp.stack([z, yl, x, core]).astype(jnp.int32)
    sequences = activations.shape[0] // SEQ * lax.axis_size("wide")

    chunk = place_in_basis(in_basis, yh)
    activations, chunk, picked = lax.optimization_barrier((activations, chunk, pick(out_basis, core)))
    mine = gather_in_basis(chunk)
    basis_own = jnp.concatenate(from_x(picked), axis=0)
    basis_flipped = other_yl(basis_own)
    acts_pieces = from_x(activations)

    top = jnp.max(jnp.abs(jnp.stack([jnp.max(jnp.abs(piece)) for piece in acts_pieces])))
    depth = NX * activations.shape[1]
    power = power_of(top.astype(F32) * (8.0 * depth))
    power_theirs = flip_yl(jnp.broadcast_to(power, (8, 128)))[0, 0]
    acts = arrange(pos, acts_pieces)
    mine, acts, basis_flipped, power_theirs = lax.optimization_barrier((mine, acts, basis_flipped, power_theirs))

    other = other_core(mine)
    basis = jnp.concatenate([basis_own, basis_flipped], axis=0)
    basis_other = other_core(basis)
    half = basis.shape[0] // 2
    out_mine = rotate_out(pos, out_grads, basis_own, basis_flipped)
    out_other = rotate_out(pos, out_grads, basis_other[:half], basis_other[half:])

    columns = mine.shape[1]
    width = columns // 2
    theirs = []
    for start in range(0, columns, width):
        given = partial(1, start, width, pos, acts, mine, other)
        got = flip_yl((given * jnp.exp2(14.0 - power)).astype(F16))
        theirs.append(got.astype(F32) * jnp.exp2(power_theirs - 14.0))
    rotated_in = partial(0, 0, columns, pos, acts, mine, other) + jnp.concatenate(theirs, axis=1)
    masked_in = rotated_in.astype(BF16) * valid.astype(BF16)[:, None]
    total = other_core(squares(pos, out_other, masked_in)) + squares(pos, out_mine, masked_in)
    return scatter_sum(total) / sequences


def solution(mesh):
    in_specs = (
        P("wide", "narrow"),
        P("wide", None),
        P("wide", "narrow"),
        P("narrow", None),
        P("wide"),
    )
    out_specs = P("wide", "narrow")
    return jax.shard_map(shards, mesh=mesh, in_specs=in_specs, out_specs=out_specs, check_vma=False)
```

```python
import functools

import jax
import jax.numpy as jnp
import numpy as np
from jax import lax
from jax.experimental import pallas as pl
from jax.experimental.pallas import tpu as pltpu
from jax.sharding import PartitionSpec as P

SEQ = 128
NZ, NYH, NC, NYL, NX = 8, 4, 2, 2, 4
BOTH = ("wide", "narrow")
F32, BF16, F16 = jnp.float32, jnp.bfloat16, jnp.float16
VMEM = pl.BlockSpec(memory_space=pltpu.VMEM)
SMEM = pl.BlockSpec(memory_space=pltpu.SMEM)
LIMIT = 48 * 1024 * 1024


def send(value, target):
    pairs = []
    for z, yh, c, yl, x in np.ndindex(NZ, NYH, NC, NYL, NX):
        z2, yh2, c2, yl2, x2 = target(z, yh, c, yl, x)
        z2, yh2, c2, yl2, x2 = z2 % NZ, yh2 % NYH, c2 % NC, yl2 % NYL, x2 % NX
        source = (((z * NYH + yh) * NC + c) * NYL + yl) * NX + x
        pairs.append((source, (((z2 * NYH + yh2) * NC + c2) * NYL + yl2) * NX + x2))
    return lax.ppermute(value, BOTH, pairs)


def other_core(value):
    return send(value, lambda z, yh, c, yl, x: (z, yh, c + 1, yl, x))


def cost(flops, nbytes):
    return pl.CostEstimate(flops=flops, bytes_accessed=nbytes, transcendentals=0)


def call(kernel, out, scratch, flops, nbytes, n_vmem):
    return pl.pallas_call(
        kernel,
        out_shape=out,
        in_specs=[SMEM] + [VMEM] * n_vmem,
        out_specs=VMEM,
        scratch_shapes=scratch,
        compiler_params=pltpu.CompilerParams(vmem_limit_bytes=LIMIT),
        cost_estimate=cost(flops, nbytes),
    )


def rotate_out_kernel(pos, grads, own, flipped, out, basis):
    rows = own.shape[0] // NX
    for ref, yl in ((own, pos[1]), (flipped, 1 - pos[1])):
        for d in range(NX):
            at = pl.multiple_of((yl * NX + lax.rem(pos[2] - d + NX, NX)) * rows, 64)
            basis[pl.ds(at, rows), :] = ref[d * rows : (d + 1) * rows, :]
    width = 256
    for j in range(out.shape[1] // width):
        cols = slice(j * width, (j + 1) * width)
        out[:, cols] = jnp.dot(grads[...], basis[:, cols], preferred_element_type=F32).astype(out.dtype)


def rotate_out(pos, grads, own, flipped):
    tokens, depth = grads.shape
    width = own.shape[1]
    return call(
        rotate_out_kernel,
        jax.ShapeDtypeStruct((tokens, width), BF16),
        [pltpu.VMEM((depth, width), BF16)],
        2 * tokens * depth * width,
        2 * (tokens * depth + depth * width + tokens * width),
        3,
    )(pos, grads, own, flipped)


def half_product(acts, basis, core):
    chunk = basis.shape[0] // NZ
    total = jnp.zeros((acts.shape[0], basis.shape[1]), F32)
    for z in range(NZ):
        at = pl.multiple_of((z * NC + core) * chunk, chunk)
        total += jnp.dot(
            acts[:, pl.ds(at, chunk)], basis[z * chunk : (z + 1) * chunk, :], preferred_element_type=F32
        )
    return total


def first_half_kernel(pos, acts, mine, out):
    out[...] = half_product(acts, mine, pos[3])


def first_half(pos, acts, mine):
    tokens, depth = acts.shape
    width = mine.shape[1]
    return call(
        first_half_kernel,
        jax.ShapeDtypeStruct((tokens, width), F32),
        [],
        tokens * depth * width,
        2 * (tokens * depth + depth * width // 2) + 4 * tokens * width,
        2,
    )(pos, acts, mine)


def masked_kernel(pos, acts, other, first, mask, out):
    total = first[...] + half_product(acts, other, 1 - pos[3])
    out[...] = (total.astype(BF16).astype(F32) * mask[...]).astype(BF16)


def masked(pos, acts, other, first, mask):
    tokens, depth = acts.shape
    width = other.shape[1]
    return call(
        masked_kernel,
        jax.ShapeDtypeStruct((tokens, width), BF16),
        [],
        tokens * depth * width,
        2 * (tokens * depth + depth * width // 2) + 6 * tokens * width,
        4,
    )(pos, acts, other, first, mask)


def squares_kernel(pos, outs, ins, out):
    width = 256
    for j in range(out.shape[0] // width):
        cols = slice(j * width, (j + 1) * width)
        total = None
        for s in range(outs.shape[0] // SEQ):
            rows = slice(s * SEQ, (s + 1) * SEQ)
            grad = lax.dot_general(
                outs[rows, cols], ins[rows, :], (((0,), (0,)), ((), ())), preferred_element_type=F32
            )
            total = grad * grad if total is None else total + grad * grad
        out[cols, :] = total


def squares(pos, outs, ins):
    tokens, width = outs.shape
    return call(
        squares_kernel,
        jax.ShapeDtypeStruct((width, ins.shape[1]), F32),
        [],
        2 * tokens * width * ins.shape[1],
        2 * tokens * (width + ins.shape[1]) + 4 * width * ins.shape[1],
        2,
    )(pos, outs, ins)


def place_in_basis(in_basis, yh):
    rows = in_basis.shape[0]

    def to(j):
        def target(z, yh, c, yl, x):
            i = (yh % 2) * 2 + c
            return z, i - j, yh // 2, yl, x

        return target

    got = [send(in_basis, to(j)) for j in range(NYH)]
    return lax.dynamic_slice_in_dim(
        jnp.concatenate(got + got, axis=0), lax.rem(NYH - yh, NYH) * rows, NYH * rows, 0
    )


def gather_in_basis(chunk):
    groups = [[z * NYH * NC + r for z in range(NZ)] for r in range(NYH * NC)]
    copies = jnp.broadcast_to(chunk[None], (NZ, *chunk.shape))
    return lax.all_to_all(copies, "wide", 0, 0, axis_index_groups=groups).reshape(-1, chunk.shape[1])


def from_x(value):
    pieces = [value]
    for d in range(1, NX):
        pieces.append(send(value, functools.partial(lambda d, z, yh, c, yl, x: (z, yh, c, yl, x + d), d)))
    return pieces


def other_yl(value):
    half = value.shape[0] // 2
    up = lambda z, yh, c, yl, x: (z, yh + yl, c, yl + 1, x)
    down = lambda z, yh, c, yl, x: (z, yh + yl - 1, c, yl + 1, x)
    return jnp.concatenate([send(value[:half], up), send(value[half:], down)], axis=0)


def power_of(top):
    return jnp.maximum(jnp.floor(jnp.log2(jnp.maximum(top, 1e-30))), -100.0)


def pick(out_basis, core):
    width = out_basis.shape[1]
    own = width // (NZ * NYH * NC)
    source = lax.broadcasted_iota(jnp.int32, (width, width // NC), 0)
    place = lax.broadcasted_iota(jnp.int32, (width, width // NC), 1)
    wanted = ((place // own) * NC + core) * own + place % own
    return jnp.dot(out_basis, (source == wanted).astype(BF16), preferred_element_type=F32).astype(BF16)


def scatter_sum(total):
    blocks = NZ * NYH
    groups = [[zy * NC + c for zy in range(blocks)] for c in range(NC)]
    rows, columns = total.shape[0] // blocks, total.shape[1]
    tiles = (rows // 8, columns // 128)
    power = power_of(jnp.max(total))
    coded = (total * jnp.exp2(14.0 - power)).astype(F16)
    coded = coded.reshape(blocks, tiles[0], 8, tiles[1], 128).transpose(0, 1, 3, 2, 4).reshape(blocks, -1, 128)
    label = jnp.broadcast_to(power.astype(F16), (blocks, 8, 128))
    got = lax.all_to_all(
        jnp.concatenate([coded, label], axis=1), "wide", 0, 0, tiled=True, axis_index_groups=groups
    )
    scale = jnp.exp2(got[:, -8:-7, :1].astype(F32) - 14.0)
    summed = jnp.sum(got[:, :-8, :].astype(F32) * scale, axis=0)
    return summed.reshape(tiles[0], tiles[1], 8, 128).transpose(0, 2, 1, 3).reshape(rows, columns)


def shards(activations, out_grads, in_basis, out_basis, valid):
    wide, narrow = lax.axis_index("wide"), lax.axis_index("narrow")
    z, yh, core = wide // (NYH * NC), (wide // NC) % NYH, wide % NC
    yl, x = narrow // NX, narrow % NX
    pos = jnp.stack([z, yl, x, core]).astype(jnp.int32)
    sequences = activations.shape[0] // SEQ * lax.axis_size("wide")

    in_basis, picked = lax.optimization_barrier((in_basis, pick(out_basis, core)))
    basis_own = jnp.concatenate(from_x(picked), axis=0)
    chunk = place_in_basis(in_basis, yh)
    activations, basis_own, chunk = lax.optimization_barrier((activations, basis_own, chunk))
    acts = lax.all_gather(activations, "narrow", axis=1, tiled=True)
    mine = gather_in_basis(chunk)
    basis_flipped = other_yl(basis_own)
    basis = jnp.concatenate([basis_own, basis_flipped], axis=0)
    basis_other = other_core(basis)
    half = basis.shape[0] // 2
    out_mine = rotate_out(pos, out_grads, basis_own, basis_flipped)
    out_other = rotate_out(pos, out_grads, basis_other[:half], basis_other[half:])
    mask = valid.astype(F32)[:, None]
    other = other_core(mine)
    masked_in = masked(pos, acts, other, first_half(pos, acts, mine), mask)
    total = other_core(squares(pos, out_other, masked_in)) + squares(pos, out_mine, masked_in)
    return scatter_sum(total) / sequences


def solution(mesh):
    in_specs = (
        P("wide", "narrow"),
        P("wide", None),
        P("wide", "narrow"),
        P("narrow", None),
        P("wide"),
    )
    out_specs = P("wide", "narrow")
    return jax.shard_map(shards, mesh=mesh, in_specs=in_specs, out_specs=out_specs, check_vma=False)
```

```python
import functools

import jax
import jax.numpy as jnp
import numpy as np
from jax import lax
from jax.experimental import pallas as pl
from jax.experimental.pallas import tpu as pltpu
from jax.sharding import PartitionSpec as P

SEQ = 128
NZ, NYH, NC, NYL, NX = 8, 4, 2, 2, 4
BOTH = ("wide", "narrow")
F32, BF16, F16 = jnp.float32, jnp.bfloat16, jnp.float16
VMEM = pl.BlockSpec(memory_space=pltpu.VMEM)
SMEM = pl.BlockSpec(memory_space=pltpu.SMEM)
LIMIT = 48 * 1024 * 1024


def send(value, target):
    pairs = []
    for z, yh, c, yl, x in np.ndindex(NZ, NYH, NC, NYL, NX):
        z2, yh2, c2, yl2, x2 = target(z, yh, c, yl, x)
        z2, yh2, c2, yl2, x2 = z2 % NZ, yh2 % NYH, c2 % NC, yl2 % NYL, x2 % NX
        source = (((z * NYH + yh) * NC + c) * NYL + yl) * NX + x
        pairs.append((source, (((z2 * NYH + yh2) * NC + c2) * NYL + yl2) * NX + x2))
    return lax.ppermute(value, BOTH, pairs)


def other_core(value):
    return send(value, lambda z, yh, c, yl, x: (z, yh, c + 1, yl, x))


def cost(flops, nbytes):
    return pl.CostEstimate(flops=flops, bytes_accessed=nbytes, transcendentals=0)


def call(kernel, out, scratch, flops, nbytes, n_vmem):
    return pl.pallas_call(
        kernel,
        out_shape=out,
        in_specs=[SMEM] + [VMEM] * n_vmem,
        out_specs=VMEM,
        scratch_shapes=scratch,
        compiler_params=pltpu.CompilerParams(vmem_limit_bytes=LIMIT),
        cost_estimate=cost(flops, nbytes),
    )


def rotate_out_kernel(pos, grads, own, flipped, out, basis):
    rows = own.shape[0] // NX
    for ref, yl in ((own, pos[1]), (flipped, 1 - pos[1])):
        for d in range(NX):
            at = pl.multiple_of((yl * NX + lax.rem(pos[2] - d + NX, NX)) * rows, 64)
            basis[pl.ds(at, rows), :] = ref[d * rows : (d + 1) * rows, :]
    width = 256
    for j in range(out.shape[1] // width):
        cols = slice(j * width, (j + 1) * width)
        out[:, cols] = jnp.dot(grads[...], basis[:, cols], preferred_element_type=F32).astype(out.dtype)


def rotate_out(pos, grads, own, flipped):
    tokens, depth = grads.shape
    width = own.shape[1]
    return call(
        rotate_out_kernel,
        jax.ShapeDtypeStruct((tokens, width), BF16),
        [pltpu.VMEM((depth, width), BF16)],
        2 * tokens * depth * width,
        2 * (tokens * depth + depth * width + tokens * width),
        3,
    )(pos, grads, own, flipped)


def arrange_kernel(pos, *refs):
    pieces, out = refs[:NX], refs[NX]
    x = pos[2]
    half = out.shape[2] // NX
    for d in range(NX):
        at = pl.multiple_of(lax.rem(x - d + NX, NX) * half, half)
        for c in range(NC):
            out[c, :, pl.ds(at, half)] = pieces[d][:, c * half : (c + 1) * half]


def arrange(pos, pieces):
    tokens, width = pieces[0].shape
    return call(
        arrange_kernel,
        jax.ShapeDtypeStruct((NC, tokens, NX * width // NC), BF16),
        [],
        0,
        4 * tokens * NX * width,
        NX,
    )(pos, *pieces)


def partial_kernel(flip, start, pos, acts, mine, other, out):
    core = pos[3]
    depth = acts.shape[2]
    rows = pl.ds(pl.multiple_of(lax.rem(pos[1] + flip, NYL) * depth, depth), depth)
    width = 256
    for j in range(out.shape[1] // width):
        here = slice(j * width, (j + 1) * width)
        cols = slice(start + j * width, start + (j + 1) * width)
        out[:, here] = jnp.dot(acts[core], mine[rows, cols], preferred_element_type=F32) + jnp.dot(
            acts[1 - core], other[rows, cols], preferred_element_type=F32
        )


def partial(flip, start, width, pos, acts, mine, other):
    tokens, depth = acts.shape[1], NC * acts.shape[2]
    return call(
        functools.partial(partial_kernel, flip, start),
        jax.ShapeDtypeStruct((tokens, width), F32),
        [],
        2 * tokens * depth * width,
        2 * (tokens * depth + depth * width) + 4 * tokens * width,
        3,
    )(pos, acts, mine, other)


def squares_kernel(pos, outs, ins, out):
    width = 256
    for j in range(out.shape[0] // width):
        cols = slice(j * width, (j + 1) * width)
        total = None
        for s in range(outs.shape[0] // SEQ):
            rows = slice(s * SEQ, (s + 1) * SEQ)
            grad = lax.dot_general(
                outs[rows, cols], ins[rows, :], (((0,), (0,)), ((), ())), preferred_element_type=F32
            )
            total = grad * grad if total is None else total + grad * grad
        out[cols, :] = total


def squares(pos, outs, ins):
    tokens, width = outs.shape
    return call(
        squares_kernel,
        jax.ShapeDtypeStruct((width, ins.shape[1]), F32),
        [],
        2 * tokens * width * ins.shape[1],
        2 * tokens * (width + ins.shape[1]) + 4 * width * ins.shape[1],
        2,
    )(pos, outs, ins)


def place_in_basis(in_basis, yh):
    rows = in_basis.shape[0]

    def to(j):
        def target(z, yh, c, yl, x):
            i = (yh % 2) * 2 + c
            return yl * (NZ // 2) + z % (NZ // 2), i - j, yh // 2, z // (NZ // 2), x

        return target

    got = [send(in_basis, to(j)) for j in range(NYH)]
    return lax.dynamic_slice_in_dim(
        jnp.concatenate(got + got, axis=0), lax.rem(NYH - yh, NYH) * rows, NYH * rows, 0
    )


def gather_in_basis(chunk):
    groups = [[z * NYH * NC + r for z in range(NZ)] for r in range(NYH * NC)]
    return lax.all_gather(chunk, "wide", axis=0, tiled=True, axis_index_groups=groups)


def from_x(value):
    pieces = [value]
    for d in range(1, NX):
        pieces.append(send(value, functools.partial(lambda d, z, yh, c, yl, x: (z, yh, c, yl, x + d), d)))
    return pieces


def flip_yl(value):
    return send(value, lambda z, yh, c, yl, x: (z, yh, c, yl + 1, x))


def other_yl(value):
    half = value.shape[0] // 2
    up = lambda z, yh, c, yl, x: (z, yh + yl, c, yl + 1, x)
    down = lambda z, yh, c, yl, x: (z, yh + yl - 1, c, yl + 1, x)
    return jnp.concatenate([send(value[:half], up), send(value[half:], down)], axis=0)


def power_of(top):
    return jnp.maximum(jnp.floor(jnp.log2(jnp.maximum(top, 1e-30))), -100.0)


def pick(out_basis, core):
    width = out_basis.shape[1]
    own = width // (NZ * NYH * NC)
    source = lax.broadcasted_iota(jnp.int32, (width, width // NC), 0)
    place = lax.broadcasted_iota(jnp.int32, (width, width // NC), 1)
    wanted = ((place // own) * NC + core) * own + place % own
    return jnp.dot(out_basis, (source == wanted).astype(BF16), preferred_element_type=F32).astype(BF16)


def scatter_sum(total):
    blocks = NZ * NYH
    groups = [[zy * NC + c for zy in range(blocks)] for c in range(NC)]
    rows, columns = total.shape[0] // blocks, total.shape[1]
    tiles = (rows // 8, columns // 128)
    power = power_of(jnp.max(total))
    coded = (total * jnp.exp2(14.0 - power)).astype(F16)
    coded = coded.reshape(blocks, tiles[0], 8, tiles[1], 128).transpose(0, 1, 3, 2, 4).reshape(blocks, -1, 128)
    label = jnp.broadcast_to(power.astype(F16), (blocks, 8, 128))
    got = lax.all_to_all(
        jnp.concatenate([coded, label], axis=1), "wide", 0, 0, tiled=True, axis_index_groups=groups
    )
    scale = jnp.exp2(got[:, -8:-7, :1].astype(F32) - 14.0)
    summed = jnp.sum(got[:, :-8, :].astype(F32) * scale, axis=0)
    return summed.reshape(tiles[0], tiles[1], 8, 128).transpose(0, 2, 1, 3).reshape(rows, columns)


def shards(activations, out_grads, in_basis, out_basis, valid):
    wide, narrow = lax.axis_index("wide"), lax.axis_index("narrow")
    z, yh, core = wide // (NYH * NC), (wide // NC) % NYH, wide % NC
    yl, x = narrow // NX, narrow % NX
    pos = jnp.stack([z, yl, x, core]).astype(jnp.int32)
    sequences = activations.shape[0] // SEQ * lax.axis_size("wide")

    chunk = place_in_basis(in_basis, yh)
    picked, chunk = lax.optimization_barrier((pick(out_basis, core), chunk))
    mine = gather_in_basis(chunk)
    basis_own = jnp.concatenate(from_x(picked), axis=0)
    activations, basis_own = lax.optimization_barrier((activations, basis_own))
    acts_pieces = from_x(activations)
    basis_flipped = other_yl(basis_own)
    basis = jnp.concatenate([basis_own, basis_flipped], axis=0)
    basis_other = other_core(basis)
    half = basis.shape[0] // 2
    out_mine = rotate_out(pos, out_grads, basis_own, basis_flipped)
    out_other = rotate_out(pos, out_grads, basis_other[:half], basis_other[half:])
    acts = arrange(pos, acts_pieces)
    top = jnp.max(jnp.abs(acts)).astype(F32)
    power = power_of(top * (8.0 * NX * activations.shape[1]))
    scale = jnp.exp2(14.0 - power)
    mine, acts, scale = lax.optimization_barrier((mine, acts, scale))

    other = other_core(mine)
    columns = mine.shape[1]
    width = columns // 2
    label = jnp.broadcast_to(power, (8, width)).astype(F16)
    theirs = []
    for start in range(0, columns, width):
        given = partial(1, start, width, pos, acts, mine, other)
        got = flip_yl(jnp.concatenate([(given * scale).astype(F16), label], axis=0))
        theirs.append(got[:-8].astype(F32) * jnp.exp2(got[-8:-7, :1].astype(F32) - 14.0))
    rotated_in = partial(0, 0, columns, pos, acts, mine, other) + jnp.concatenate(theirs, axis=1)
    masked_in = rotated_in.astype(BF16) * valid.astype(BF16)[:, None]
    total = other_core(squares(pos, out_other, masked_in)) + squares(pos, out_mine, masked_in)
    return scatter_sum(total) / sequences


def solution(mesh):
    in_specs = (
        P("wide", "narrow"),
        P("wide", None),
        P("wide", "narrow"),
        P("narrow", None),
        P("wide"),
    )
    out_specs = P("wide", "narrow")
    return jax.shard_map(shards, mesh=mesh, in_specs=in_specs, out_specs=out_specs, check_vma=False)
```

```python
import functools

import jax
import jax.numpy as jnp
import numpy as np
from jax import lax
from jax.experimental import pallas as pl
from jax.experimental.pallas import tpu as pltpu
from jax.sharding import PartitionSpec as P

SEQ = 128
NZ, NYH, NC, NYL, NX = 8, 4, 2, 2, 4
BOTH = ("wide", "narrow")
F32, BF16, F16 = jnp.float32, jnp.bfloat16, jnp.float16
VMEM = pl.BlockSpec(memory_space=pltpu.VMEM)
SMEM = pl.BlockSpec(memory_space=pltpu.SMEM)
LIMIT = 48 * 1024 * 1024


def send(value, target):
    pairs = []
    for z, yh, c, yl, x in np.ndindex(NZ, NYH, NC, NYL, NX):
        z2, yh2, c2, yl2, x2 = target(z, yh, c, yl, x)
        z2, yh2, c2, yl2, x2 = z2 % NZ, yh2 % NYH, c2 % NC, yl2 % NYL, x2 % NX
        source = (((z * NYH + yh) * NC + c) * NYL + yl) * NX + x
        pairs.append((source, (((z2 * NYH + yh2) * NC + c2) * NYL + yl2) * NX + x2))
    return lax.ppermute(value, BOTH, pairs)


def other_core(value):
    return send(value, lambda z, yh, c, yl, x: (z, yh, c + 1, yl, x))


def cost(flops, nbytes):
    return pl.CostEstimate(flops=flops, bytes_accessed=nbytes, transcendentals=0)


def call(kernel, out, scratch, flops, nbytes, n_vmem):
    return pl.pallas_call(
        kernel,
        out_shape=out,
        in_specs=[SMEM] + [VMEM] * n_vmem,
        out_specs=VMEM,
        scratch_shapes=scratch,
        compiler_params=pltpu.CompilerParams(vmem_limit_bytes=LIMIT),
        cost_estimate=cost(flops, nbytes),
    )


def rotate_out_kernel(pos, grads, packed, out, basis):
    parts = NYL * NX
    rows, stride = basis.shape[0] // parts, packed.shape[0] // parts
    wide = packed.shape[1]
    for n in range(parts):
        at, half = n * stride, rows // 2
        basis[n * rows : (n + 1) * rows, :wide] = packed[at : at + rows, :]
        for h in range(2):
            basis[n * rows + h * half : n * rows + (h + 1) * half, wide:] = packed[
                at + rows : at + stride, h * wide // 2 : (h + 1) * wide // 2
            ]
    width = 256
    for j in range(out.shape[1] // width):
        cols = slice(j * width, (j + 1) * width)
        out[:, cols] = jnp.dot(grads[...], basis[:, cols], preferred_element_type=F32).astype(out.dtype)


def rotate_out(pos, grads, packed):
    tokens, depth = grads.shape
    width = depth // NC
    return call(
        rotate_out_kernel,
        jax.ShapeDtypeStruct((tokens, width), BF16),
        [pltpu.VMEM((depth, width), BF16)],
        2 * tokens * depth * width,
        2 * (tokens * depth + depth * width + tokens * width),
        2,
    )(pos, grads, packed)


def rotate_in_kernel(pos, gathered, mine, other, mask, out, basis):
    core = pos[3]
    blocks = NZ * NYH
    rows = mine.shape[0] // blocks
    for i in range(blocks):
        for ref, c in ((mine, core), (other, 1 - core)):
            at = pl.multiple_of((i * NC + c) * rows, rows)
            basis[pl.ds(at, rows), :] = ref[i * rows : (i + 1) * rows, :]
    parts = NYL * NX
    stride, depth = gathered.shape[0] // parts, gathered.shape[1]
    half = out.shape[0] // 2
    for part in range(2):
        total = jnp.zeros((half, out.shape[1]), F32)
        for n in range(parts):
            at = n * stride + part * half
            total += jnp.dot(
                gathered[at : at + half, :], basis[n * depth : (n + 1) * depth, :], preferred_element_type=F32
            )
        here = slice(part * half, (part + 1) * half)
        out[here, :] = (total.astype(BF16).astype(F32) * mask[here, :]).astype(BF16)


def rotate_in(pos, gathered, mine, other, mask):
    tokens = mask.shape[0]
    depth, width = 2 * mine.shape[0], mine.shape[1]
    return call(
        rotate_in_kernel,
        jax.ShapeDtypeStruct((tokens, width), BF16),
        [pltpu.VMEM((depth, width), BF16)],
        2 * tokens * depth * width,
        2 * (tokens * depth + depth * width + tokens * width),
        4,
    )(pos, gathered, mine, other, mask)


def squares_kernel(pos, outs, ins, out):
    width = 256
    for j in range(out.shape[0] // width):
        cols = slice(j * width, (j + 1) * width)
        total = None
        for s in range(outs.shape[0] // SEQ):
            rows = slice(s * SEQ, (s + 1) * SEQ)
            grad = lax.dot_general(
                outs[rows, cols], ins[rows, :], (((0,), (0,)), ((), ())), preferred_element_type=F32
            )
            total = grad * grad if total is None else total + grad * grad
        out[cols, :] = total


def squares(pos, outs, ins):
    tokens, width = outs.shape
    return call(
        squares_kernel,
        jax.ShapeDtypeStruct((width, ins.shape[1]), F32),
        [],
        2 * tokens * width * ins.shape[1],
        2 * tokens * (width + ins.shape[1]) + 4 * width * ins.shape[1],
        2,
    )(pos, outs, ins)


def gather_in_basis(in_basis):
    along_yh = [[(z * NYH + yh) * NC + c for yh in range(NYH)] for z in range(NZ) for c in range(NC)]
    along_z = [[z * NYH * NC + r for z in range(NZ)] for r in range(NYH * NC)]
    chunk = lax.all_gather(in_basis, "wide", axis=0, tiled=True, axis_index_groups=along_yh)
    copies = jnp.broadcast_to(chunk[None], (NZ, *chunk.shape))
    return lax.all_to_all(copies, "wide", 0, 0, axis_index_groups=along_z).reshape(-1, chunk.shape[1])


def gather_packed(activations, picked):
    width = activations.shape[1]
    half = picked.shape[0] // 2
    rest = jnp.concatenate([picked[:half, width:], picked[half:, width:]], axis=1)
    packed = jnp.concatenate([activations, picked[:, :width], rest], axis=0)
    return lax.all_gather(packed, "narrow", axis=0, tiled=True)


def power_of(top):
    return jnp.maximum(jnp.floor(jnp.log2(jnp.maximum(top, 1e-30))), -100.0)


def pick(out_basis, core):
    width = out_basis.shape[1]
    own = width // (NZ * NYH * NC)
    source = lax.broadcasted_iota(jnp.int32, (width, width // NC), 0)
    place = lax.broadcasted_iota(jnp.int32, (width, width // NC), 1)
    wanted = ((place // own) * NC + core) * own + place % own
    return jnp.dot(out_basis, (source == wanted).astype(BF16), preferred_element_type=F32).astype(BF16)


def scatter_sum(total):
    blocks = NZ * NYH
    groups = [[zy * NC + c for zy in range(blocks)] for c in range(NC)]
    rows, columns = total.shape[0] // blocks, total.shape[1]
    tiles = (rows // 8, columns // 128)
    power = power_of(jnp.max(total))
    coded = (total * jnp.exp2(14.0 - power)).astype(F16)
    coded = coded.reshape(blocks, tiles[0], 8, tiles[1], 128).transpose(0, 1, 3, 2, 4).reshape(blocks, -1, 128)
    label = jnp.broadcast_to(power.astype(F16), (blocks, 8, 128))
    got = lax.all_to_all(
        jnp.concatenate([coded, label], axis=1), "wide", 0, 0, tiled=True, axis_index_groups=groups
    )
    scale = jnp.exp2(got[:, -8:-7, :1].astype(F32) - 14.0)
    summed = jnp.sum(got[:, :-8, :].astype(F32) * scale, axis=0)
    return summed.reshape(tiles[0], tiles[1], 8, 128).transpose(0, 2, 1, 3).reshape(rows, columns)


def shards(activations, out_grads, in_basis, out_basis, valid):
    wide, narrow = lax.axis_index("wide"), lax.axis_index("narrow")
    z, yh, core = wide // (NYH * NC), (wide // NC) % NYH, wide % NC
    yl, x = narrow // NX, narrow % NX
    pos = jnp.stack([z, yl, x, core]).astype(jnp.int32)
    sequences = activations.shape[0] // SEQ * lax.axis_size("wide")

    gathered = gather_packed(activations, pick(out_basis, core))
    mine = gather_in_basis(in_basis)
    other = other_core(mine)
    parts = NYL * NX
    basis = gathered.reshape(parts, -1, gathered.shape[1])[:, activations.shape[0] :]
    basis = basis.reshape(-1, gathered.shape[1])
    basis_other = other_core(basis)
    mask = valid.astype(F32)[:, None]
    out_mine = rotate_out(pos, out_grads, basis)
    masked_in = rotate_in(pos, gathered, mine, other, mask)
    out_other = rotate_out(pos, out_grads, basis_other)
    total = other_core(squares(pos, out_other, masked_in)) + squares(pos, out_mine, masked_in)
    return scatter_sum(total) / sequences


def solution(mesh):
    in_specs = (
        P("wide", "narrow"),
        P("wide", None),
        P("wide", "narrow"),
        P("narrow", None),
        P("wide"),
    )
    out_specs = P("wide", "narrow")
    return jax.shard_map(shards, mesh=mesh, in_specs=in_specs, out_specs=out_specs, check_vma=False)
```

```python
import functools

import jax
import jax.numpy as jnp
import numpy as np
from jax import lax
from jax.experimental import pallas as pl
from jax.experimental.pallas import tpu as pltpu
from jax.sharding import PartitionSpec as P

SEQ = 128
NZ, NYH, NC, NYL, NX = 8, 4, 2, 2, 4
BOTH = ("wide", "narrow")
F32, BF16, F16 = jnp.float32, jnp.bfloat16, jnp.float16
VMEM = pl.BlockSpec(memory_space=pltpu.VMEM)
SMEM = pl.BlockSpec(memory_space=pltpu.SMEM)
LIMIT = 48 * 1024 * 1024


def send(value, target):
    pairs = []
    for z, yh, c, yl, x in np.ndindex(NZ, NYH, NC, NYL, NX):
        z2, yh2, c2, yl2, x2 = target(z, yh, c, yl, x)
        z2, yh2, c2, yl2, x2 = z2 % NZ, yh2 % NYH, c2 % NC, yl2 % NYL, x2 % NX
        source = (((z * NYH + yh) * NC + c) * NYL + yl) * NX + x
        pairs.append((source, (((z2 * NYH + yh2) * NC + c2) * NYL + yl2) * NX + x2))
    return lax.ppermute(value, BOTH, pairs)


def other_core(value):
    return send(value, lambda z, yh, c, yl, x: (z, yh, c + 1, yl, x))


def cost(flops, nbytes):
    return pl.CostEstimate(flops=flops, bytes_accessed=nbytes, transcendentals=0)


def call(kernel, out, scratch, flops, nbytes, n_vmem):
    return pl.pallas_call(
        kernel,
        out_shape=out,
        in_specs=[SMEM] + [VMEM] * n_vmem,
        out_specs=VMEM,
        scratch_shapes=scratch,
        compiler_params=pltpu.CompilerParams(vmem_limit_bytes=LIMIT),
        cost_estimate=cost(flops, nbytes),
    )


def rotate_out_kernel(pos, grads, packed, out, basis):
    parts = NYL * NX
    rows, stride = basis.shape[0] // parts, packed.shape[0] // parts
    wide, half = packed.shape[1], rows // 2
    skip = stride - rows - half
    for n in range(parts):
        at = n * stride + skip
        basis[n * rows : (n + 1) * rows, :wide] = packed[at : at + rows, :]
        for h in range(2):
            basis[n * rows + h * half : n * rows + (h + 1) * half, wide:] = packed[
                at + rows : at + rows + half, h * wide // 2 : (h + 1) * wide // 2
            ]
    width = 256
    for j in range(out.shape[1] // width):
        cols = slice(j * width, (j + 1) * width)
        out[:, cols] = jnp.dot(grads[...], basis[:, cols], preferred_element_type=F32).astype(out.dtype)


def rotate_out(pos, grads, packed):
    tokens, depth = grads.shape
    width = depth // NC
    return call(
        rotate_out_kernel,
        jax.ShapeDtypeStruct((tokens, width), BF16),
        [pltpu.VMEM((depth, width), BF16)],
        2 * tokens * depth * width,
        2 * (tokens * depth + depth * width + tokens * width),
        2,
    )(pos, grads, packed)


def rotate_in_kernel(pos, gathered, mine, other, mask, out, basis):
    core = pos[3]
    blocks = NZ * NYH
    rows = mine.shape[0] // blocks
    for i in range(blocks):
        for ref, c in ((mine, core), (other, 1 - core)):
            at = pl.multiple_of((i * NC + c) * rows, rows)
            basis[pl.ds(at, rows), :] = ref[i * rows : (i + 1) * rows, :]
    parts = NYL * NX
    stride, depth = gathered.shape[0] // parts, gathered.shape[1]
    half = out.shape[0] // 2
    for part in range(2):
        total = jnp.zeros((half, out.shape[1]), F32)
        for n in range(parts):
            at = n * stride + part * half
            total += jnp.dot(
                gathered[at : at + half, :], basis[n * depth : (n + 1) * depth, :], preferred_element_type=F32
            )
        here = slice(part * half, (part + 1) * half)
        out[here, :] = (total.astype(BF16).astype(F32) * mask[here, :]).astype(BF16)


def rotate_in(pos, gathered, mine, other, mask):
    tokens = mask.shape[0]
    depth, width = 2 * mine.shape[0], mine.shape[1]
    return call(
        rotate_in_kernel,
        jax.ShapeDtypeStruct((tokens, width), BF16),
        [pltpu.VMEM((depth, width), BF16)],
        2 * tokens * depth * width,
        2 * (tokens * depth + depth * width + tokens * width),
        4,
    )(pos, gathered, mine, other, mask)


def squares_kernel(pos, outs, ins, *refs):
    before, out = refs[:-1], refs[-1]
    width = 256
    for j in range(out.shape[0] // width):
        cols = slice(j * width, (j + 1) * width)
        total = before[0][cols, :] if before else None
        for s in range(outs.shape[0] // SEQ):
            rows = slice(s * SEQ, (s + 1) * SEQ)
            grad = lax.dot_general(
                outs[rows, cols], ins[rows, :], (((0,), (0,)), ((), ())), preferred_element_type=F32
            )
            total = grad * grad if total is None else total + grad * grad
        out[cols, :] = total


def squares(pos, outs, ins, *before):
    tokens, width = outs.shape
    return call(
        squares_kernel,
        jax.ShapeDtypeStruct((width, ins.shape[1]), F32),
        [],
        2 * tokens * width * ins.shape[1],
        2 * tokens * (width + ins.shape[1]) + 4 * width * ins.shape[1],
        2 + len(before),
    )(pos, outs, ins, *before)


def gather_in_basis(in_basis):
    along_yh = [[(z * NYH + yh) * NC + c for yh in range(NYH)] for z in range(NZ) for c in range(NC)]
    along_z = [[z * NYH * NC + r for z in range(NZ)] for r in range(NYH * NC)]
    chunk = lax.all_gather(in_basis, "wide", axis=0, tiled=True, axis_index_groups=along_yh)
    copies = jnp.broadcast_to(chunk[None], (NZ, *chunk.shape))
    return lax.all_to_all(copies, "wide", 0, 0, axis_index_groups=along_z).reshape(-1, chunk.shape[1])


def gather_packed(activations, picked):
    width = activations.shape[1]
    half = picked.shape[0] // 2
    rest = jnp.concatenate([picked[:half, width:], picked[half:, width:]], axis=1)
    packed = jnp.concatenate([activations, picked[:, :width], rest], axis=0)
    return lax.all_gather(packed, "narrow", axis=0, tiled=True)


def power_of(top):
    return jnp.maximum(jnp.floor(jnp.log2(jnp.maximum(top, 1e-30))), -100.0)


def pick(out_basis, core):
    width = out_basis.shape[1]
    own = width // (NZ * NYH * NC)
    source = lax.broadcasted_iota(jnp.int32, (width, width // NC), 0)
    place = lax.broadcasted_iota(jnp.int32, (width, width // NC), 1)
    wanted = ((place // own) * NC + core) * own + place % own
    return jnp.dot(out_basis, (source == wanted).astype(BF16), preferred_element_type=F32).astype(BF16)


def scatter_sum(total):
    blocks = NZ * NYH
    groups = [[zy * NC + c for zy in range(blocks)] for c in range(NC)]
    rows, columns = total.shape[0] // blocks, total.shape[1]
    tiles = (rows // 8, columns // 128)
    power = power_of(jnp.max(total))
    coded = (total * jnp.exp2(14.0 - power)).astype(F16)
    coded = coded.reshape(blocks, tiles[0], 8, tiles[1], 128).transpose(0, 1, 3, 2, 4).reshape(blocks, -1, 128)
    label = jnp.broadcast_to(power.astype(F16), (blocks, 8, 128))
    got = lax.all_to_all(
        jnp.concatenate([coded, label], axis=1), "wide", 0, 0, tiled=True, axis_index_groups=groups
    )
    scale = jnp.exp2(got[:, -8:-7, :1].astype(F32) - 14.0)
    summed = jnp.sum(got[:, :-8, :].astype(F32) * scale, axis=0)
    return summed.reshape(tiles[0], tiles[1], 8, 128).transpose(0, 2, 1, 3).reshape(rows, columns)


def shards(activations, out_grads, in_basis, out_basis, valid):
    wide, narrow = lax.axis_index("wide"), lax.axis_index("narrow")
    z, yh, core = wide // (NYH * NC), (wide // NC) % NYH, wide % NC
    yl, x = narrow // NX, narrow % NX
    pos = jnp.stack([z, yl, x, core]).astype(jnp.int32)
    sequences = activations.shape[0] // SEQ * lax.axis_size("wide")

    gathered = gather_packed(activations, pick(out_basis, core))
    mine = gather_in_basis(in_basis)
    grads_other = other_core(out_grads)
    other = other_core(mine)
    gathered, other, grads_other = lax.optimization_barrier((gathered, other, grads_other))
    mask = valid.astype(F32)[:, None]
    masked_in = rotate_in(pos, gathered, mine, other, mask)
    masked_other = other_core(masked_in)
    out_mine = rotate_out(pos, out_grads, gathered)
    out_theirs = rotate_out(pos, grads_other, gathered)
    total = squares(pos, out_theirs, masked_other, squares(pos, out_mine, masked_in))
    return scatter_sum(total) / sequences


def solution(mesh):
    in_specs = (
        P("wide", "narrow"),
        P("wide", None),
        P("wide", "narrow"),
        P("narrow", None),
        P("wide"),
    )
    out_specs = P("wide", "narrow")
    return jax.shard_map(shards, mesh=mesh, in_specs=in_specs, out_specs=out_specs, check_vma=False)
```

```python
import functools

import jax
import jax.numpy as jnp
import numpy as np
from jax import lax
from jax.experimental import pallas as pl
from jax.experimental.pallas import tpu as pltpu
from jax.sharding import PartitionSpec as P

SEQ = 128
NZ, NYH, NC, NYL, NX = 8, 4, 2, 2, 4
BOTH = ("wide", "narrow")
F32, BF16, F16 = jnp.float32, jnp.bfloat16, jnp.float16
VMEM = pl.BlockSpec(memory_space=pltpu.VMEM)
SMEM = pl.BlockSpec(memory_space=pltpu.SMEM)
LIMIT = 48 * 1024 * 1024


def send(value, target):
    pairs = []
    for z, yh, c, yl, x in np.ndindex(NZ, NYH, NC, NYL, NX):
        z2, yh2, c2, yl2, x2 = target(z, yh, c, yl, x)
        z2, yh2, c2, yl2, x2 = z2 % NZ, yh2 % NYH, c2 % NC, yl2 % NYL, x2 % NX
        source = (((z * NYH + yh) * NC + c) * NYL + yl) * NX + x
        pairs.append((source, (((z2 * NYH + yh2) * NC + c2) * NYL + yl2) * NX + x2))
    return lax.ppermute(value, BOTH, pairs)


def other_core(value):
    return send(value, lambda z, yh, c, yl, x: (z, yh, c + 1, yl, x))


def cost(flops, nbytes):
    return pl.CostEstimate(flops=flops, bytes_accessed=nbytes, transcendentals=0)


def rotate_in_kernel(pos, gathered, mine, other, mask, out, basis, total, plane):
    n, core = pl.program_id(0), pos[3]
    tokens, rows = out.shape[0], mine.shape[0] // NYH
    for i in range(NYH):
        for ref, c in ((mine, core), (other, 1 - core)):
            at = pl.multiple_of((i * NC + c) * rows, rows)
            plane[pl.ds(at, rows), :] = ref[i * rows : (i + 1) * rows, :]
    product = jnp.dot(gathered[:tokens, :], plane[...], preferred_element_type=F32)

    @pl.when(n == 0)
    def _():
        total[...] = product

    @pl.when(n > 0)
    def _():
        total[...] += product

    @pl.when(n == pl.num_programs(0) - 1)
    def _():
        out[...] = (total[...].astype(BF16).astype(F32) * mask[...]).astype(BF16)

    height, wide = basis.shape[0], gathered.shape[1]
    half, at = height // 2, tokens + height
    basis[:, :wide] = gathered[tokens:at, :]
    for h in range(2):
        basis[h * half : (h + 1) * half, wide:] = gathered[at:, h * wide // 2 : (h + 1) * wide // 2]


def rotate_in(pos, gathered, mine, other, mask, basis_shape):
    parts = NYL * NX
    tokens, width = mask.shape[0], mine.shape[1]
    depth = 2 * mine.shape[0]
    by_rows = lambda array: pl.BlockSpec((array.shape[0] // parts, array.shape[1]), lambda n: (n, 0))
    basis = jax.ShapeDtypeStruct(basis_shape, BF16)
    return pl.pallas_call(
        rotate_in_kernel,
        grid=(parts,),
        out_shape=[jax.ShapeDtypeStruct((tokens, width), BF16), basis],
        in_specs=[
            SMEM,
            by_rows(gathered),
            by_rows(mine),
            by_rows(other),
            pl.BlockSpec(mask.shape, lambda n: (0, 0)),
        ],
        out_specs=[pl.BlockSpec((tokens, width), lambda n: (0, 0)), by_rows(basis)],
        scratch_shapes=[pltpu.VMEM((tokens, width), F32), pltpu.VMEM((depth // parts, width), BF16)],
        compiler_params=pltpu.CompilerParams(vmem_limit_bytes=LIMIT),
        cost_estimate=cost(2 * tokens * depth * width, 2 * (gathered.size + 2 * mine.size + tokens * width)),
    )(pos, gathered, mine, other, mask)


def rotate_out_kernel(mine, theirs, basis, out_mine, out_theirs):
    width = 256
    for j in range(basis.shape[1] // width):
        cols = slice(j * width, (j + 1) * width)
        for grads, out in ((mine, out_mine), (theirs, out_theirs)):
            out[:, cols] = jnp.dot(grads[...], basis[:, cols], preferred_element_type=F32).astype(BF16)


def rotate_out(mine, theirs, basis):
    tokens, depth = mine.shape
    width = basis.shape[1]
    return pl.pallas_call(
        rotate_out_kernel,
        out_shape=[jax.ShapeDtypeStruct((tokens, width), BF16)] * 2,
        in_specs=[VMEM] * 3,
        out_specs=[VMEM] * 2,
        compiler_params=pltpu.CompilerParams(vmem_limit_bytes=LIMIT),
        cost_estimate=cost(4 * tokens * depth * width, 2 * (2 * tokens * (depth + width) + depth * width)),
    )(mine, theirs, basis)


def squares_kernel(outs_mine, outs_theirs, ins_mine, ins_theirs, out, top):
    width = 256
    for j in range(out.shape[0] // width):
        cols = slice(j * width, (j + 1) * width)
        total = None
        for outs, ins in ((outs_mine, ins_mine), (outs_theirs, ins_theirs)):
            for s in range(outs.shape[0] // SEQ):
                rows = slice(s * SEQ, (s + 1) * SEQ)
                grad = lax.dot_general(
                    outs[rows, cols], ins[rows, :], (((0,), (0,)), ((), ())), preferred_element_type=F32
                )
                total = grad * grad if total is None else total + grad * grad
        out[cols, :] = total
        largest = jnp.max(total.reshape(width // 8, 8, out.shape[1]), axis=0)
        top[...] = largest if j == 0 else jnp.maximum(top[...], largest)


def squares(outs_mine, outs_theirs, ins_mine, ins_theirs):
    tokens, width = outs_mine.shape
    columns = ins_mine.shape[1]
    return pl.pallas_call(
        squares_kernel,
        out_shape=[jax.ShapeDtypeStruct((width, columns), F32), jax.ShapeDtypeStruct((8, columns), F32)],
        in_specs=[VMEM] * 4,
        out_specs=[VMEM] * 2,
        compiler_params=pltpu.CompilerParams(vmem_limit_bytes=LIMIT),
        cost_estimate=cost(4 * tokens * width * columns, 4 * tokens * (width + columns) + 4 * width * columns),
    )(outs_mine, outs_theirs, ins_mine, ins_theirs)


def gather_in_basis(in_basis):
    along_yh = [[(z * NYH + yh) * NC + c for yh in range(NYH)] for z in range(NZ) for c in range(NC)]
    along_z = [[z * NYH * NC + r for z in range(NZ)] for r in range(NYH * NC)]
    chunk = lax.all_gather(in_basis, "wide", axis=0, tiled=True, axis_index_groups=along_yh)
    copies = jnp.broadcast_to(chunk[None], (NZ, *chunk.shape))
    return lax.all_to_all(copies, "wide", 0, 0, axis_index_groups=along_z).reshape(-1, chunk.shape[1])


def gather_packed(activations, picked):
    width = activations.shape[1]
    half = picked.shape[0] // 2
    rest = jnp.concatenate([picked[:half, width:], picked[half:, width:]], axis=1)
    packed = jnp.concatenate([activations, picked[:, :width], rest], axis=0)
    return lax.all_gather(packed, "narrow", axis=0, tiled=True)


def power_of(top):
    return jnp.maximum(jnp.floor(jnp.log2(jnp.maximum(top, 1e-30))), -100.0)


def pick(out_basis, core):
    width = out_basis.shape[1]
    own = width // (NZ * NYH * NC)
    source = lax.broadcasted_iota(jnp.int32, (width, width // NC), 0)
    place = lax.broadcasted_iota(jnp.int32, (width, width // NC), 1)
    wanted = ((place // own) * NC + core) * own + place % own
    return jnp.dot(out_basis, (source == wanted).astype(BF16), preferred_element_type=F32).astype(BF16)


def scatter_sum(total, top):
    blocks = NZ * NYH
    groups = [[zy * NC + c for zy in range(blocks)] for c in range(NC)]
    rows, columns = total.shape[0] // blocks, total.shape[1]
    tiles = (rows // 8, columns // 128)
    power = power_of(top)
    coded = (total * jnp.exp2(14.0 - power)).astype(F16)
    coded = coded.reshape(blocks, tiles[0], 8, tiles[1], 128).transpose(0, 1, 3, 2, 4).reshape(blocks, -1, 128)
    label = jnp.broadcast_to(power.astype(F16), (blocks, 8, 128))
    got = lax.all_to_all(
        jnp.concatenate([coded, label], axis=1), "wide", 0, 0, tiled=True, axis_index_groups=groups
    )
    scale = jnp.exp2(got[:, -8:-7, :1].astype(F32) - 14.0)
    summed = jnp.sum(got[:, :-8, :].astype(F32) * scale, axis=0)
    return summed.reshape(tiles[0], tiles[1], 8, 128).transpose(0, 2, 1, 3).reshape(rows, columns)


def shards(activations, out_grads, in_basis, out_basis, valid):
    wide, narrow = lax.axis_index("wide"), lax.axis_index("narrow")
    z, yh, core = wide // (NYH * NC), (wide // NC) % NYH, wide % NC
    yl, x = narrow // NX, narrow % NX
    pos = jnp.stack([z, yl, x, core]).astype(jnp.int32)
    sequences = activations.shape[0] // SEQ * lax.axis_size("wide")

    gathered = gather_packed(activations, pick(out_basis, core))
    mine = gather_in_basis(in_basis)
    grads_other = other_core(out_grads)
    other = other_core(mine)
    gathered, other, grads_other = lax.optimization_barrier((gathered, other, grads_other))
    mask = valid.astype(F32)[:, None]
    basis_shape = (out_basis.shape[1], out_basis.shape[1] // NC)
    masked_in, basis = rotate_in(pos, gathered, mine, other, mask, basis_shape)
    masked_other = other_core(masked_in)
    out_mine, out_theirs = rotate_out(out_grads, grads_other, basis)
    total, top = squares(out_mine, out_theirs, masked_in, masked_other)
    return scatter_sum(total, jnp.max(top)) / sequences


def solution(mesh):
    in_specs = (
        P("wide", "narrow"),
        P("wide", None),
        P("wide", "narrow"),
        P("narrow", None),
        P("wide"),
    )
    out_specs = P("wide", "narrow")
    return jax.shard_map(shards, mesh=mesh, in_specs=in_specs, out_specs=out_specs, check_vma=False)
```

```python
import functools

import jax
import jax.numpy as jnp
import numpy as np
from jax import lax
from jax.experimental import pallas as pl
from jax.experimental.pallas import tpu as pltpu
from jax.sharding import PartitionSpec as P

SEQ = 128
NZ, NYH, NC, NYL, NX = 8, 4, 2, 2, 4
BOTH = ("wide", "narrow")
F32, BF16, F16 = jnp.float32, jnp.bfloat16, jnp.float16
VMEM = pl.BlockSpec(memory_space=pltpu.VMEM)
SMEM = pl.BlockSpec(memory_space=pltpu.SMEM)
ANY = pl.BlockSpec(memory_space=pl.ANY)
LIMIT = 48 * 1024 * 1024


def send(value, target):
    pairs = []
    for z, yh, c, yl, x in np.ndindex(NZ, NYH, NC, NYL, NX):
        z2, yh2, c2, yl2, x2 = target(z, yh, c, yl, x)
        z2, yh2, c2, yl2, x2 = z2 % NZ, yh2 % NYH, c2 % NC, yl2 % NYL, x2 % NX
        source = (((z * NYH + yh) * NC + c) * NYL + yl) * NX + x
        pairs.append((source, (((z2 * NYH + yh2) * NC + c2) * NYL + yl2) * NX + x2))
    return lax.ppermute(value, BOTH, pairs)


def other_core(value):
    return send(value, lambda z, yh, c, yl, x: (z, yh, c + 1, yl, x))


def cost(flops, nbytes):
    return pl.CostEstimate(flops=flops, bytes_accessed=nbytes, transcendentals=0)


def rotate_in_kernel(pos, gathered, mine, other, mask, out, blocks, basis, sems):
    core, parts = pos[3], blocks.shape[0]
    stride, (tokens, depth) = gathered.shape[0] // parts, blocks.shape[1:]
    copies = [
        pltpu.make_async_copy(gathered.at[pl.ds(n * stride, tokens), :], blocks.at[n], sems.at[n])
        for n in range(parts)
    ]
    for copy in copies:
        copy.start()
    rows = mine.shape[0] // (NZ * NYH)
    for i in range(NZ * NYH):
        for ref, c in ((mine, core), (other, 1 - core)):
            at = pl.multiple_of((i * NC + c) * rows, rows)
            basis[pl.ds(at, rows), :] = ref[i * rows : (i + 1) * rows, :]
    half = tokens // 2
    for part in range(2):
        here = slice(part * half, (part + 1) * half)
        total = jnp.zeros((half, out.shape[1]), F32)
        for n in range(parts):
            if part == 0:
                copies[n].wait()
            total += jnp.dot(
                blocks[n, here, :], basis[n * depth : (n + 1) * depth, :], preferred_element_type=F32
            )
        out[here, :] = (total.astype(BF16).astype(F32) * mask[here, :]).astype(BF16)


def rotate_in(pos, gathered, mine, other, mask):
    parts = NYL * NX
    tokens, width = mask.shape[0], mine.shape[1]
    depth = 2 * mine.shape[0]
    return pl.pallas_call(
        rotate_in_kernel,
        out_shape=jax.ShapeDtypeStruct((tokens, width), BF16),
        in_specs=[SMEM, ANY, VMEM, VMEM, VMEM],
        out_specs=VMEM,
        scratch_shapes=[
            pltpu.VMEM((parts, tokens, depth // parts), BF16),
            pltpu.VMEM((depth, width), BF16),
            pltpu.SemaphoreType.DMA((parts,)),
        ],
        compiler_params=pltpu.CompilerParams(vmem_limit_bytes=LIMIT),
        cost_estimate=cost(2 * tokens * depth * width, 2 * (tokens * depth + depth * width + tokens * width)),
    )(pos, gathered, mine, other, mask)


def rotate_out_kernel(gathered, mine, theirs, out_mine, out_theirs, basis, sems):
    parts = NYL * NX
    stride, wide = gathered.shape[0] // parts, gathered.shape[1]
    height = basis.shape[0] // parts
    half, rest = height // 2, basis.shape[1] - wide
    copies = []
    for n in range(parts):
        at = (n + 1) * stride - half - height
        pieces = [(at, height, 0, wide, n * height, 0)]
        for h in range(2):
            pieces.append((at + height, half, h * rest, rest, n * height + h * half, wide))
        for row, rows, col, cols, to_row, to_col in pieces:
            copies.append(
                pltpu.make_async_copy(
                    gathered.at[pl.ds(row, rows), pl.ds(col, cols)],
                    basis.at[pl.ds(to_row, rows), pl.ds(to_col, cols)],
                    sems.at[len(copies)],
                )
            )
    for copy in copies:
        copy.start()
    for copy in copies:
        copy.wait()
    width = 256
    for j in range(basis.shape[1] // width):
        cols = slice(j * width, (j + 1) * width)
        for grads, out in ((mine, out_mine), (theirs, out_theirs)):
            out[:, cols] = jnp.dot(grads[...], basis[:, cols], preferred_element_type=F32).astype(BF16)


def rotate_out(gathered, mine, theirs):
    tokens, depth = mine.shape
    width = depth // NC
    return pl.pallas_call(
        rotate_out_kernel,
        out_shape=[jax.ShapeDtypeStruct((tokens, width), BF16)] * 2,
        in_specs=[ANY, VMEM, VMEM],
        out_specs=[VMEM] * 2,
        scratch_shapes=[pltpu.VMEM((depth, width), BF16), pltpu.SemaphoreType.DMA((3 * NYL * NX,))],
        compiler_params=pltpu.CompilerParams(vmem_limit_bytes=LIMIT),
        cost_estimate=cost(4 * tokens * depth * width, 2 * (2 * tokens * (depth + width) + depth * width)),
    )(gathered, mine, theirs)


def squares_kernel(outs_mine, outs_theirs, ins_mine, ins_theirs, out, top):
    width = 256
    for j in range(out.shape[0] // width):
        cols = slice(j * width, (j + 1) * width)
        total = None
        for outs, ins in ((outs_mine, ins_mine), (outs_theirs, ins_theirs)):
            for s in range(outs.shape[0] // SEQ):
                rows = slice(s * SEQ, (s + 1) * SEQ)
                grad = lax.dot_general(
                    outs[rows, cols], ins[rows, :], (((0,), (0,)), ((), ())), preferred_element_type=F32
                )
                total = grad * grad if total is None else total + grad * grad
        out[cols, :] = total
        largest = jnp.max(total.reshape(width // 8, 8, out.shape[1]), axis=0)
        top[...] = largest if j == 0 else jnp.maximum(top[...], largest)


def squares(outs_mine, outs_theirs, ins_mine, ins_theirs):
    tokens, width = outs_mine.shape
    columns = ins_mine.shape[1]
    return pl.pallas_call(
        squares_kernel,
        out_shape=[jax.ShapeDtypeStruct((width, columns), F32), jax.ShapeDtypeStruct((8, columns), F32)],
        in_specs=[VMEM] * 4,
        out_specs=[VMEM] * 2,
        compiler_params=pltpu.CompilerParams(vmem_limit_bytes=LIMIT),
        cost_estimate=cost(4 * tokens * width * columns, 4 * tokens * (width + columns) + 4 * width * columns),
    )(outs_mine, outs_theirs, ins_mine, ins_theirs)


def gather_in_basis(in_basis, grads):
    along_yh = [[(z * NYH + yh) * NC + c for yh in range(NYH)] for z in range(NZ) for c in range(NC)]
    along_z = [[z * NYH * NC + r for z in range(NZ)] for r in range(NYH * NC)]
    chunk = lax.all_gather(in_basis, "wide", axis=0, tiled=True, axis_index_groups=along_yh)
    chunk, grads = lax.optimization_barrier((chunk, other_core(grads)))
    copies = jnp.broadcast_to(chunk[None], (NZ, *chunk.shape))
    got = lax.all_to_all(copies, "wide", 0, 0, axis_index_groups=along_z)
    return got.reshape(-1, chunk.shape[1]), grads


def gather_packed(activations, picked):
    width = activations.shape[1]
    half = picked.shape[0] // 2
    rest = jnp.concatenate([picked[:half, width:], picked[half:, width:]], axis=1)
    packed = jnp.concatenate([activations, picked[:, :width], rest], axis=0)
    return lax.all_gather(packed, "narrow", axis=0, tiled=True)


def power_of(top):
    return jnp.maximum(jnp.floor(jnp.log2(jnp.maximum(top, 1e-30))), -100.0)


def pick(out_basis, core):
    width = out_basis.shape[1]
    own = width // (NZ * NYH * NC)
    source = lax.broadcasted_iota(jnp.int32, (width, width // NC), 0)
    place = lax.broadcasted_iota(jnp.int32, (width, width // NC), 1)
    wanted = ((place // own) * NC + core) * own + place % own
    return jnp.dot(out_basis, (source == wanted).astype(BF16), preferred_element_type=F32).astype(BF16)


def scatter_sum(total, top):
    blocks = NZ * NYH
    groups = [[zy * NC + c for zy in range(blocks)] for c in range(NC)]
    rows, columns = total.shape[0] // blocks, total.shape[1]
    tiles = (rows // 8, columns // 128)
    power = power_of(top)
    coded = (total * jnp.exp2(14.0 - power)).astype(F16)
    coded = coded.reshape(blocks, tiles[0], 8, tiles[1], 128).transpose(0, 1, 3, 2, 4).reshape(blocks, -1, 128)
    label = jnp.broadcast_to(power.astype(F16), (blocks, 8, 128))
    got = lax.all_to_all(
        jnp.concatenate([coded, label], axis=1), "wide", 0, 0, tiled=True, axis_index_groups=groups
    )
    scale = jnp.exp2(got[:, -8:-7, :1].astype(F32) - 14.0)
    summed = jnp.sum(got[:, :-8, :].astype(F32) * scale, axis=0)
    return summed.reshape(tiles[0], tiles[1], 8, 128).transpose(0, 2, 1, 3).reshape(rows, columns)


def shards(activations, out_grads, in_basis, out_basis, valid):
    wide, narrow = lax.axis_index("wide"), lax.axis_index("narrow")
    z, yh, core = wide // (NYH * NC), (wide // NC) % NYH, wide % NC
    yl, x = narrow // NX, narrow % NX
    pos = jnp.stack([z, yl, x, core]).astype(jnp.int32)
    sequences = activations.shape[0] // SEQ * lax.axis_size("wide")

    gathered = gather_packed(activations, pick(out_basis, core))
    mine, grads_other = gather_in_basis(in_basis, out_grads)
    other = other_core(mine)
    gathered, other = lax.optimization_barrier((gathered, other))
    mask = valid.astype(F32)[:, None]
    masked_in = rotate_in(pos, gathered, mine, other, mask)
    masked_other = other_core(masked_in)
    out_mine, out_theirs = rotate_out(gathered, out_grads, grads_other)
    total, top = squares(out_mine, out_theirs, masked_in, masked_other)
    return scatter_sum(total, jnp.max(top)) / sequences


def solution(mesh):
    in_specs = (
        P("wide", "narrow"),
        P("wide", None),
        P("wide", "narrow"),
        P("narrow", None),
        P("wide"),
    )
    out_specs = P("wide", "narrow")
    return jax.shard_map(shards, mesh=mesh, in_specs=in_specs, out_specs=out_specs, check_vma=False)
```

```python
import functools

import jax
import jax.numpy as jnp
import numpy as np
from jax import lax
from jax.experimental import pallas as pl
from jax.experimental.pallas import tpu as pltpu
from jax.sharding import PartitionSpec as P

SEQ = 128
NZ, NYH, NC, NYL, NX = 8, 4, 2, 2, 4
BOTH = ("wide", "narrow")
F32, BF16, F16 = jnp.float32, jnp.bfloat16, jnp.float16
VMEM = pl.BlockSpec(memory_space=pltpu.VMEM)
SMEM = pl.BlockSpec(memory_space=pltpu.SMEM)
ANY = pl.BlockSpec(memory_space=pl.ANY)
LIMIT = 48 * 1024 * 1024


def send(value, target):
    pairs = []
    for z, yh, c, yl, x in np.ndindex(NZ, NYH, NC, NYL, NX):
        z2, yh2, c2, yl2, x2 = target(z, yh, c, yl, x)
        z2, yh2, c2, yl2, x2 = z2 % NZ, yh2 % NYH, c2 % NC, yl2 % NYL, x2 % NX
        source = (((z * NYH + yh) * NC + c) * NYL + yl) * NX + x
        pairs.append((source, (((z2 * NYH + yh2) * NC + c2) * NYL + yl2) * NX + x2))
    return lax.ppermute(value, BOTH, pairs)


def other_core(value):
    return send(value, lambda z, yh, c, yl, x: (z, yh, c + 1, yl, x))


def cost(flops, nbytes):
    return pl.CostEstimate(flops=flops, bytes_accessed=nbytes, transcendentals=0)


def rotate_in_kernel(pos, gathered, mine, mine_next, other, other_next, mask, out, blocks, basis, sems):
    parity, core, parts = lax.rem(pos[0], 2), pos[3], blocks.shape[0]
    stride, (tokens, depth) = gathered.shape[0] // parts, blocks.shape[1:]
    copies = [
        pltpu.make_async_copy(gathered.at[pl.ds(n * stride, tokens), :], blocks.at[n], sems.at[n])
        for n in range(parts)
    ]
    for copy in copies:
        copy.start()
    rows = basis.shape[0] // (NZ * NYH * NC)
    for ref, c, first in ((mine, core, 0), (mine_next, core, 1), (other, 1 - core, 0), (other_next, 1 - core, 1)):
        odd = lax.rem(parity + first, 2)
        for i in range(NZ // 2 * NYH):
            z, yh = 2 * (i // NYH) + odd, i % NYH
            at = pl.multiple_of(((z * NYH + yh) * NC + c) * rows, rows)
            basis[pl.ds(at, rows), :] = ref[i * rows : (i + 1) * rows, :]
    width = 256
    for j in range(out.shape[1] // width):
        cols = slice(j * width, (j + 1) * width)
        total = jnp.zeros((tokens, width), F32)
        for n in range(parts):
            if j == 0:
                copies[n].wait()
            total += jnp.dot(blocks[n], basis[n * depth : (n + 1) * depth, cols], preferred_element_type=F32)
        out[:, cols] = (total.astype(BF16).astype(F32) * mask[...]).astype(BF16)


def rotate_in(pos, gathered, planes, mask):
    parts = NYL * NX
    tokens, width = mask.shape[0], planes[0].shape[1]
    depth = len(planes) * planes[0].shape[0]
    return pl.pallas_call(
        rotate_in_kernel,
        out_shape=jax.ShapeDtypeStruct((tokens, width), BF16),
        in_specs=[SMEM, ANY] + [VMEM] * 5,
        out_specs=VMEM,
        scratch_shapes=[
            pltpu.VMEM((parts, tokens, depth // parts), BF16),
            pltpu.VMEM((depth, width), BF16),
            pltpu.SemaphoreType.DMA((parts,)),
        ],
        compiler_params=pltpu.CompilerParams(vmem_limit_bytes=LIMIT),
        cost_estimate=cost(2 * tokens * depth * width, 2 * (tokens * depth + depth * width + tokens * width)),
    )(pos, gathered, *planes, mask)


def rotate_out_kernel(pos, gathered, below, above, mine, theirs, out_mine, out_theirs, basis, sems):
    parity, parts = lax.rem(pos[0], 2), NYL * NX
    wide = gathered.shape[1]
    height = basis.shape[0] // parts // 2
    half, rest = height // 2, basis.shape[1] - wide
    stride, packed = gathered.shape[0] // parts, height + half
    copies = []
    for n in range(parts):
        near = below if n < parts // 2 else above
        for ref, at, q in (
            (gathered, (n + 1) * stride - packed, parity),
            (near, n % (parts // 2) * packed, 1 - parity),
        ):
            top = (2 * n + q) * height
            pieces = [(at, height, 0, wide, top, 0)]
            for h in range(2):
                pieces.append((at + height, half, h * rest, rest, top + h * half, wide))
            for row, rows, col, cols, to_row, to_col in pieces:
                copies.append(
                    pltpu.make_async_copy(
                        ref.at[pl.ds(row, rows), pl.ds(col, cols)],
                        basis.at[pl.ds(pl.multiple_of(to_row, 16), rows), pl.ds(to_col, cols)],
                        sems.at[len(copies)],
                    )
                )
    for copy in copies:
        copy.start()
    for copy in copies:
        copy.wait()
    width = 256
    for j in range(basis.shape[1] // width):
        cols = slice(j * width, (j + 1) * width)
        for grads, out in ((mine, out_mine), (theirs, out_theirs)):
            out[:, cols] = jnp.dot(grads[...], basis[:, cols], preferred_element_type=F32).astype(BF16)


def rotate_out(pos, gathered, below, above, mine, theirs):
    tokens, depth = mine.shape
    width = depth // NC
    return pl.pallas_call(
        rotate_out_kernel,
        out_shape=[jax.ShapeDtypeStruct((tokens, width), BF16)] * 2,
        in_specs=[SMEM, ANY, ANY, ANY, VMEM, VMEM],
        out_specs=[VMEM] * 2,
        scratch_shapes=[pltpu.VMEM((depth, width), BF16), pltpu.SemaphoreType.DMA((6 * NYL * NX,))],
        compiler_params=pltpu.CompilerParams(vmem_limit_bytes=LIMIT),
        cost_estimate=cost(4 * tokens * depth * width, 2 * (2 * tokens * (depth + width) + depth * width)),
    )(pos, gathered, below, above, mine, theirs)


def squares_kernel(outs_mine, outs_theirs, ins_mine, ins_theirs, out, top):
    width = 256
    for j in range(out.shape[0] // width):
        cols = slice(j * width, (j + 1) * width)
        total = None
        for outs, ins in ((outs_mine, ins_mine), (outs_theirs, ins_theirs)):
            for s in range(outs.shape[0] // SEQ):
                rows = slice(s * SEQ, (s + 1) * SEQ)
                grad = lax.dot_general(
                    outs[rows, cols], ins[rows, :], (((0,), (0,)), ((), ())), preferred_element_type=F32
                )
                total = grad * grad if total is None else total + grad * grad
        out[cols, :] = total
        largest = jnp.max(total.reshape(width // 8, 8, out.shape[1]), axis=0)
        top[...] = largest if j == 0 else jnp.maximum(top[...], largest)


def squares(outs_mine, outs_theirs, ins_mine, ins_theirs):
    tokens, width = outs_mine.shape
    columns = ins_mine.shape[1]
    return pl.pallas_call(
        squares_kernel,
        out_shape=[jax.ShapeDtypeStruct((width, columns), F32), jax.ShapeDtypeStruct((8, columns), F32)],
        in_specs=[VMEM] * 4,
        out_specs=[VMEM] * 2,
        compiler_params=pltpu.CompilerParams(vmem_limit_bytes=LIMIT),
        cost_estimate=cost(4 * tokens * width * columns, 4 * tokens * (width + columns) + 4 * width * columns),
    )(outs_mine, outs_theirs, ins_mine, ins_theirs)


def to_all(value, groups):
    copies = jnp.broadcast_to(value[None], (len(groups[0]), *value.shape))
    return lax.all_to_all(copies, "wide", 0, 0, axis_index_groups=groups).reshape(-1, value.shape[1])


def from_z_neighbours(value):
    half = value.shape[0] // 2
    below = send(value[:half], lambda z, yh, c, yl, x: (z + 1, yh, c, yl, x))
    above = send(value[half:], lambda z, yh, c, yl, x: (z - 1, yh, c, yl, x))
    return below, above


def gather_in_basis(in_basis, grads):
    along_yh = [[(z * NYH + yh) * NC + c for yh in range(NYH)] for z in range(NZ) for c in range(NC)]
    along_z = [[z * NYH * NC + r for z in range(p, NZ, 2)] for p in range(2) for r in range(NYH * NC)]
    chunk = to_all(in_basis, along_yh)
    chunk, grads = lax.optimization_barrier((chunk, other_core(grads)))
    planes = to_all(chunk, along_z)
    following = jnp.concatenate(from_z_neighbours(planes), axis=0)
    return (planes, following, other_core(planes), other_core(following)), grads


def gather_packed(activations, picked):
    width = activations.shape[1]
    half = picked.shape[0] // 2
    rest = jnp.concatenate([picked[:half, width:], picked[half:, width:]], axis=1)
    packed = jnp.concatenate([activations, picked[:, :width], rest], axis=0)
    return lax.all_gather(packed, "narrow", axis=0, tiled=True)


def power_of(top):
    return jnp.maximum(jnp.floor(jnp.log2(jnp.maximum(top, 1e-30))), -100.0)


def pick(out_basis, core):
    width = out_basis.shape[1]
    own = width // (NZ * NYH * NC)
    source = lax.broadcasted_iota(jnp.int32, (width, width // NC), 0)
    place = lax.broadcasted_iota(jnp.int32, (width, width // NC), 1)
    wanted = ((place // own) * NC + core) * own + place % own
    return jnp.dot(out_basis, (source == wanted).astype(BF16), preferred_element_type=F32).astype(BF16)


def scatter_sum(total, top):
    blocks = NZ * NYH
    groups = [[zy * NC + c for zy in range(blocks)] for c in range(NC)]
    rows, columns = total.shape[0] // blocks, total.shape[1]
    tiles = (rows // 8, columns // 128)
    power = power_of(top)
    coded = (total * jnp.exp2(14.0 - power)).astype(F16)
    coded = coded.reshape(blocks, tiles[0], 8, tiles[1], 128).transpose(0, 1, 3, 2, 4).reshape(blocks, -1, 128)
    label = jnp.broadcast_to(power.astype(F16), (blocks, 8, 128))
    got = lax.all_to_all(
        jnp.concatenate([coded, label], axis=1), "wide", 0, 0, tiled=True, axis_index_groups=groups
    )
    scale = jnp.exp2(got[:, -8:-7, :1].astype(F32) - 14.0)
    summed = jnp.sum(got[:, :-8, :].astype(F32) * scale, axis=0)
    return summed.reshape(tiles[0], tiles[1], 8, 128).transpose(0, 2, 1, 3).reshape(rows, columns)


def shards(activations, out_grads, in_basis, out_basis, valid):
    wide, narrow = lax.axis_index("wide"), lax.axis_index("narrow")
    z, yh, core = wide // (NYH * NC), (wide // NC) % NYH, wide % NC
    yl, x = narrow // NX, narrow % NX
    pos = jnp.stack([z, yl, x, core]).astype(jnp.int32)
    sequences = activations.shape[0] // SEQ * lax.axis_size("wide")

    height = out_basis.shape[0] // 2
    parity_rows = lax.dynamic_slice_in_dim(out_basis, lax.rem(z, 2) * height, height, 0)
    gathered = gather_packed(activations, pick(parity_rows, core))
    planes, grads_other = gather_in_basis(in_basis, out_grads)
    basis = gathered.reshape(NYL * NX, -1, gathered.shape[1])[:, activations.shape[0] :]
    below, above = from_z_neighbours(basis.reshape(-1, gathered.shape[1]))
    mask = valid.astype(F32)[:, None]
    masked_in = rotate_in(pos, gathered, planes, mask)
    masked_other = other_core(masked_in)
    out_mine, out_theirs = rotate_out(pos, gathered, below, above, out_grads, grads_other)
    total, top = squares(out_mine, out_theirs, masked_in, masked_other)
    return scatter_sum(total, jnp.max(top)) / sequences


def solution(mesh):
    in_specs = (
        P("wide", "narrow"),
        P("wide", None),
        P("wide", "narrow"),
        P("narrow", None),
        P("wide"),
    )
    out_specs = P("wide", "narrow")
    return jax.shard_map(shards, mesh=mesh, in_specs=in_specs, out_specs=out_specs, check_vma=False)
```

```python
import functools

import jax
import jax.numpy as jnp
import numpy as np
from jax import lax
from jax.experimental import pallas as pl
from jax.experimental.pallas import tpu as pltpu
from jax.sharding import PartitionSpec as P

SEQ = 128
NZ, NYH, NC, NYL, NX = 8, 4, 2, 2, 4
BOTH = ("wide", "narrow")
F32, BF16, F16 = jnp.float32, jnp.bfloat16, jnp.float16
VMEM = pl.BlockSpec(memory_space=pltpu.VMEM)
SMEM = pl.BlockSpec(memory_space=pltpu.SMEM)
ANY = pl.BlockSpec(memory_space=pl.ANY)
LIMIT = 48 * 1024 * 1024


def send(value, target):
    pairs = []
    for z, yh, c, yl, x in np.ndindex(NZ, NYH, NC, NYL, NX):
        z2, yh2, c2, yl2, x2 = target(z, yh, c, yl, x)
        z2, yh2, c2, yl2, x2 = z2 % NZ, yh2 % NYH, c2 % NC, yl2 % NYL, x2 % NX
        source = (((z * NYH + yh) * NC + c) * NYL + yl) * NX + x
        pairs.append((source, (((z2 * NYH + yh2) * NC + c2) * NYL + yl2) * NX + x2))
    return lax.ppermute(value, BOTH, pairs)


def other_core(value):
    return send(value, lambda z, yh, c, yl, x: (z, yh, c + 1, yl, x))


def cost(flops, nbytes):
    return pl.CostEstimate(flops=flops, bytes_accessed=nbytes, transcendentals=0)


def rotate_in_kernel(pos, gathered, mine, mine_next, other, other_next, mask, out, blocks, basis, sems):
    parity, core, parts = lax.rem(pos[0], 2), pos[3], blocks.shape[0]
    stride, (tokens, depth) = gathered.shape[0] // parts, blocks.shape[1:]
    copies = [
        pltpu.make_async_copy(gathered.at[pl.ds(n * stride, tokens), :], blocks.at[n], sems.at[n])
        for n in range(parts)
    ]
    for copy in copies:
        copy.start()
    rows = basis.shape[0] // (NZ * NYH * NC)
    for ref, c, first in ((mine, core, 0), (mine_next, core, 1), (other, 1 - core, 0), (other_next, 1 - core, 1)):
        odd = lax.rem(parity + first, 2)
        for i in range(NZ // 2 * NYH):
            z, yh = 2 * (i // NYH) + odd, i % NYH
            at = pl.multiple_of(((z * NYH + yh) * NC + c) * rows, rows)
            basis[pl.ds(at, rows), :] = ref[i * rows : (i + 1) * rows, :]
    half = tokens // 2
    for part in range(2):
        here = slice(part * half, (part + 1) * half)
        total = jnp.zeros((half, out.shape[1]), F32)
        for n in range(parts):
            if part == 0:
                copies[n].wait()
            total += jnp.dot(
                blocks[n, here, :], basis[n * depth : (n + 1) * depth, :], preferred_element_type=F32
            )
        out[here, :] = (total.astype(BF16).astype(F32) * mask[here, :]).astype(BF16)


def rotate_in(pos, gathered, planes, mask):
    parts = NYL * NX
    tokens, width = mask.shape[0], planes[0].shape[1]
    depth = len(planes) * planes[0].shape[0]
    return pl.pallas_call(
        rotate_in_kernel,
        out_shape=jax.ShapeDtypeStruct((tokens, width), BF16),
        in_specs=[SMEM, ANY] + [VMEM] * 5,
        out_specs=VMEM,
        scratch_shapes=[
            pltpu.VMEM((parts, tokens, depth // parts), BF16),
            pltpu.VMEM((depth, width), BF16),
            pltpu.SemaphoreType.DMA((parts,)),
        ],
        compiler_params=pltpu.CompilerParams(vmem_limit_bytes=LIMIT),
        cost_estimate=cost(2 * tokens * depth * width, 2 * (tokens * depth + depth * width + tokens * width)),
    )(pos, gathered, *planes, mask)


def rotate_out_kernel(pos, gathered, below, above, mine, theirs, out_mine, out_theirs, basis, sems):
    parity, parts = lax.rem(pos[0], 2), NYL * NX
    wide = gathered.shape[1]
    height = basis.shape[0] // parts // 2
    half, rest = height // 2, basis.shape[1] - wide
    stride, packed = gathered.shape[0] // parts, height + half
    copies = []
    for n in range(parts):
        near = below if n < parts // 2 else above
        for ref, at, q in (
            (gathered, (n + 1) * stride - packed, parity),
            (near, n % (parts // 2) * packed, 1 - parity),
        ):
            top = (2 * n + q) * height
            pieces = [(at, height, 0, wide, top, 0)]
            for h in range(2):
                pieces.append((at + height, half, h * rest, rest, top + h * half, wide))
            for row, rows, col, cols, to_row, to_col in pieces:
                copies.append(
                    pltpu.make_async_copy(
                        ref.at[pl.ds(row, rows), pl.ds(col, cols)],
                        basis.at[pl.ds(pl.multiple_of(to_row, 16), rows), pl.ds(to_col, cols)],
                        sems.at[len(copies)],
                    )
                )
    for copy in copies:
        copy.start()
    for copy in copies:
        copy.wait()
    width = 256
    for j in range(basis.shape[1] // width):
        cols = slice(j * width, (j + 1) * width)
        for grads, out in ((mine, out_mine), (theirs, out_theirs)):
            out[:, cols] = jnp.dot(grads[...], basis[:, cols], preferred_element_type=F32).astype(BF16)


def rotate_out(pos, gathered, below, above, mine, theirs):
    tokens, depth = mine.shape
    width = depth // NC
    return pl.pallas_call(
        rotate_out_kernel,
        out_shape=[jax.ShapeDtypeStruct((tokens, width), BF16)] * 2,
        in_specs=[SMEM, ANY, ANY, ANY, VMEM, VMEM],
        out_specs=[VMEM] * 2,
        scratch_shapes=[pltpu.VMEM((depth, width), BF16), pltpu.SemaphoreType.DMA((6 * NYL * NX,))],
        compiler_params=pltpu.CompilerParams(vmem_limit_bytes=LIMIT),
        cost_estimate=cost(4 * tokens * depth * width, 2 * (2 * tokens * (depth + width) + depth * width)),
    )(pos, gathered, below, above, mine, theirs)


def squares_kernel(outs_mine, outs_theirs, ins_mine, ins_theirs, out, top):
    width = 256
    for j in range(out.shape[0] // width):
        cols = slice(j * width, (j + 1) * width)
        total = None
        for outs, ins in ((outs_mine, ins_mine), (outs_theirs, ins_theirs)):
            for s in range(outs.shape[0] // SEQ):
                rows = slice(s * SEQ, (s + 1) * SEQ)
                grad = lax.dot_general(
                    outs[rows, cols], ins[rows, :], (((0,), (0,)), ((), ())), preferred_element_type=F32
                )
                total = grad * grad if total is None else total + grad * grad
        out[cols, :] = total
        largest = jnp.max(total.reshape(width // 8, 8, out.shape[1]), axis=0)
        top[...] = largest if j == 0 else jnp.maximum(top[...], largest)


def squares(outs_mine, outs_theirs, ins_mine, ins_theirs):
    tokens, width = outs_mine.shape
    columns = ins_mine.shape[1]
    return pl.pallas_call(
        squares_kernel,
        out_shape=[jax.ShapeDtypeStruct((width, columns), F32), jax.ShapeDtypeStruct((8, columns), F32)],
        in_specs=[VMEM] * 4,
        out_specs=[VMEM] * 2,
        compiler_params=pltpu.CompilerParams(vmem_limit_bytes=LIMIT),
        cost_estimate=cost(4 * tokens * width * columns, 4 * tokens * (width + columns) + 4 * width * columns),
    )(outs_mine, outs_theirs, ins_mine, ins_theirs)


def to_all(value, groups):
    copies = jnp.broadcast_to(value[None], (len(groups[0]), *value.shape))
    return lax.all_to_all(copies, "wide", 0, 0, axis_index_groups=groups).reshape(-1, value.shape[1])


def from_z_neighbours(value):
    half = value.shape[0] // 2
    below = send(value[:half], lambda z, yh, c, yl, x: (z + 1, yh, c, yl, x))
    above = send(value[half:], lambda z, yh, c, yl, x: (z - 1, yh, c, yl, x))
    return below, above


def gather_in_basis(in_basis, grads):
    along_yh = [[(z * NYH + yh) * NC + c for yh in range(NYH)] for z in range(NZ) for c in range(NC)]
    along_z = [[z * NYH * NC + r for z in range(p, NZ, 2)] for p in range(2) for r in range(NYH * NC)]
    chunk = to_all(in_basis, along_yh)
    chunk, grads = lax.optimization_barrier((chunk, other_core(grads)))
    planes = to_all(chunk, along_z)
    following = jnp.concatenate(from_z_neighbours(planes), axis=0)
    return planes, following, other_core(planes), grads


def gather_packed(activations, picked):
    width = activations.shape[1]
    half = picked.shape[0] // 2
    rest = jnp.concatenate([picked[:half, width:], picked[half:, width:]], axis=1)
    packed = jnp.concatenate([activations, picked[:, :width], rest], axis=0)
    return lax.all_gather(packed, "narrow", axis=0, tiled=True)


def power_of(top):
    return jnp.maximum(jnp.floor(jnp.log2(jnp.maximum(top, 1e-30))), -100.0)


def pick(out_basis, core):
    width = out_basis.shape[1]
    own = width // (NZ * NYH * NC)
    source = lax.broadcasted_iota(jnp.int32, (width, width // NC), 0)
    place = lax.broadcasted_iota(jnp.int32, (width, width // NC), 1)
    wanted = ((place // own) * NC + core) * own + place % own
    return jnp.dot(out_basis, (source == wanted).astype(BF16), preferred_element_type=F32).astype(BF16)


def scatter_sum(total, top):
    blocks = NZ * NYH
    groups = [[zy * NC + c for zy in range(blocks)] for c in range(NC)]
    rows, columns = total.shape[0] // blocks, total.shape[1]
    tiles = (rows // 8, columns // 128)
    power = power_of(top)
    coded = (total * jnp.exp2(14.0 - power)).astype(F16)
    coded = coded.reshape(blocks, tiles[0], 8, tiles[1], 128).transpose(0, 1, 3, 2, 4).reshape(blocks, -1, 128)
    label = jnp.broadcast_to(power.astype(F16), (blocks, 8, 128))
    got = lax.all_to_all(
        jnp.concatenate([coded, label], axis=1), "wide", 0, 0, tiled=True, axis_index_groups=groups
    )
    scale = jnp.exp2(got[:, -8:-7, :1].astype(F32) - 14.0)
    summed = jnp.sum(got[:, :-8, :].astype(F32) * scale, axis=0)
    return summed.reshape(tiles[0], tiles[1], 8, 128).transpose(0, 2, 1, 3).reshape(rows, columns)


def shards(activations, out_grads, in_basis, out_basis, valid):
    wide, narrow = lax.axis_index("wide"), lax.axis_index("narrow")
    z, yh, core = wide // (NYH * NC), (wide // NC) % NYH, wide % NC
    yl, x = narrow // NX, narrow % NX
    pos = jnp.stack([z, yl, x, core]).astype(jnp.int32)
    sequences = activations.shape[0] // SEQ * lax.axis_size("wide")

    height = out_basis.shape[0] // 2
    parity_rows = lax.dynamic_slice_in_dim(out_basis, lax.rem(z, 2) * height, height, 0)
    gathered = gather_packed(activations, pick(parity_rows, core))
    planes, following, planes_other, grads_other = gather_in_basis(in_basis, out_grads)
    basis = gathered.reshape(NYL * NX, -1, gathered.shape[1])[:, activations.shape[0] :]
    basis, following = lax.optimization_barrier((basis.reshape(-1, gathered.shape[1]), following))
    below, above = from_z_neighbours(basis)
    planes = (planes, following, planes_other, other_core(following))
    mask = valid.astype(F32)[:, None]
    masked_in = rotate_in(pos, gathered, planes, mask)
    masked_other = other_core(masked_in)
    out_mine, out_theirs = rotate_out(pos, gathered, below, above, out_grads, grads_other)
    total, top = squares(out_mine, out_theirs, masked_in, masked_other)
    return scatter_sum(total, jnp.max(top)) / sequences


def solution(mesh):
    in_specs = (
        P("wide", "narrow"),
        P("wide", None),
        P("wide", "narrow"),
        P("narrow", None),
        P("wide"),
    )
    out_specs = P("wide", "narrow")
    return jax.shard_map(shards, mesh=mesh, in_specs=in_specs, out_specs=out_specs, check_vma=False)
```

```python
import functools

import jax
import jax.numpy as jnp
import numpy as np
from jax import lax
from jax.experimental import pallas as pl
from jax.experimental.pallas import tpu as pltpu
from jax.sharding import PartitionSpec as P

SEQ = 128
NZ, NYH, NC, NYL, NX = 8, 4, 2, 2, 4
BOTH = ("wide", "narrow")
F32, BF16, F16 = jnp.float32, jnp.bfloat16, jnp.float16
VMEM = pl.BlockSpec(memory_space=pltpu.VMEM)
SMEM = pl.BlockSpec(memory_space=pltpu.SMEM)
ANY = pl.BlockSpec(memory_space=pl.ANY)
LIMIT = 48 * 1024 * 1024


def send(value, target):
    pairs = []
    for z, yh, c, yl, x in np.ndindex(NZ, NYH, NC, NYL, NX):
        z2, yh2, c2, yl2, x2 = target(z, yh, c, yl, x)
        z2, yh2, c2, yl2, x2 = z2 % NZ, yh2 % NYH, c2 % NC, yl2 % NYL, x2 % NX
        source = (((z * NYH + yh) * NC + c) * NYL + yl) * NX + x
        pairs.append((source, (((z2 * NYH + yh2) * NC + c2) * NYL + yl2) * NX + x2))
    return lax.ppermute(value, BOTH, pairs)


def other_core(value):
    return send(value, lambda z, yh, c, yl, x: (z, yh, c + 1, yl, x))


def cost(flops, nbytes):
    return pl.CostEstimate(flops=flops, bytes_accessed=nbytes, transcendentals=0)


def rotate_in_kernel(pos, gathered, mine, other, mask, out, blocks, basis, sems):
    core, parts = pos[3], blocks.shape[0]
    stride, (tokens, depth) = gathered.shape[0] // parts, blocks.shape[1:]
    copies = [
        pltpu.make_async_copy(gathered.at[pl.ds(n * stride, tokens), :], blocks.at[n], sems.at[n])
        for n in range(parts)
    ]
    for copy in copies:
        copy.start()
    rows = mine.shape[0] // (NZ * NYH)
    for i in range(NZ * NYH):
        for ref, c in ((mine, core), (other, 1 - core)):
            at = pl.multiple_of((i * NC + c) * rows, rows)
            basis[pl.ds(at, rows), :] = ref[i * rows : (i + 1) * rows, :]
    half = tokens // 2
    for part in range(2):
        here = slice(part * half, (part + 1) * half)
        total = jnp.zeros((half, out.shape[1]), F32)
        for n in range(parts):
            if part == 0:
                copies[n].wait()
            total += jnp.dot(
                blocks[n, here, :], basis[n * depth : (n + 1) * depth, :], preferred_element_type=F32
            )
        out[here, :] = (total.astype(BF16).astype(F32) * mask[here, :]).astype(BF16)


def rotate_in(pos, gathered, mine, other, mask):
    parts = NYL * NX
    tokens, width = mask.shape[0], mine.shape[1]
    depth = 2 * mine.shape[0]
    return pl.pallas_call(
        rotate_in_kernel,
        out_shape=jax.ShapeDtypeStruct((tokens, width), BF16),
        in_specs=[SMEM, ANY, VMEM, VMEM, VMEM],
        out_specs=VMEM,
        scratch_shapes=[
            pltpu.VMEM((parts, tokens, depth // parts), BF16),
            pltpu.VMEM((depth, width), BF16),
            pltpu.SemaphoreType.DMA((parts,)),
        ],
        compiler_params=pltpu.CompilerParams(vmem_limit_bytes=LIMIT),
        cost_estimate=cost(2 * tokens * depth * width, 2 * (tokens * depth + depth * width + tokens * width)),
    )(pos, gathered, mine, other, mask)


def rotate_out_kernel(gathered, mine, theirs, out_mine, out_theirs, basis, sems):
    parts = NYL * NX
    stride, wide = gathered.shape[0] // parts, gathered.shape[1]
    height = basis.shape[0] // parts
    half, rest = height // 2, basis.shape[1] - wide
    copies = []
    for n in range(parts):
        at = (n + 1) * stride - half - height
        pieces = [(at, height, 0, wide, n * height, 0)]
        for h in range(2):
            pieces.append((at + height, half, h * rest, rest, n * height + h * half, wide))
        for row, rows, col, cols, to_row, to_col in pieces:
            copies.append(
                pltpu.make_async_copy(
                    gathered.at[pl.ds(row, rows), pl.ds(col, cols)],
                    basis.at[pl.ds(to_row, rows), pl.ds(to_col, cols)],
                    sems.at[len(copies)],
                )
            )
    for copy in copies:
        copy.start()
    for copy in copies:
        copy.wait()
    width = 256
    for j in range(basis.shape[1] // width):
        cols = slice(j * width, (j + 1) * width)
        for grads, out in ((mine, out_mine), (theirs, out_theirs)):
            out[:, cols] = jnp.dot(grads[...], basis[:, cols], preferred_element_type=F32).astype(BF16)


def rotate_out(gathered, mine, theirs):
    tokens, depth = mine.shape
    width = depth // NC
    return pl.pallas_call(
        rotate_out_kernel,
        out_shape=[jax.ShapeDtypeStruct((tokens, width), BF16)] * 2,
        in_specs=[ANY, VMEM, VMEM],
        out_specs=[VMEM] * 2,
        scratch_shapes=[pltpu.VMEM((depth, width), BF16), pltpu.SemaphoreType.DMA((3 * NYL * NX,))],
        compiler_params=pltpu.CompilerParams(vmem_limit_bytes=LIMIT),
        cost_estimate=cost(4 * tokens * depth * width, 2 * (2 * tokens * (depth + width) + depth * width)),
    )(gathered, mine, theirs)


def squares_kernel(outs_mine, outs_theirs, ins_mine, ins_theirs, out, top):
    width = 256
    for j in range(out.shape[0] // width):
        cols = slice(j * width, (j + 1) * width)
        total = None
        for outs, ins in ((outs_mine, ins_mine), (outs_theirs, ins_theirs)):
            for s in range(outs.shape[0] // SEQ):
                rows = slice(s * SEQ, (s + 1) * SEQ)
                grad = lax.dot_general(
                    outs[rows, cols], ins[rows, :], (((0,), (0,)), ((), ())), preferred_element_type=F32
                )
                total = grad * grad if total is None else total + grad * grad
        out[cols, :] = total
        largest = jnp.max(total.reshape(width // 8, 8, out.shape[1]), axis=0)
        top[...] = largest if j == 0 else jnp.maximum(top[...], largest)


def squares(outs_mine, outs_theirs, ins_mine, ins_theirs):
    tokens, width = outs_mine.shape
    columns = ins_mine.shape[1]
    return pl.pallas_call(
        squares_kernel,
        out_shape=[jax.ShapeDtypeStruct((width, columns), F32), jax.ShapeDtypeStruct((8, columns), F32)],
        in_specs=[VMEM] * 4,
        out_specs=[VMEM] * 2,
        compiler_params=pltpu.CompilerParams(vmem_limit_bytes=LIMIT),
        cost_estimate=cost(4 * tokens * width * columns, 4 * tokens * (width + columns) + 4 * width * columns),
    )(outs_mine, outs_theirs, ins_mine, ins_theirs)


def gather_in_basis(in_basis, grads):
    along_yh = [[(z * NYH + yh) * NC + c for yh in range(NYH)] for z in range(NZ) for c in range(NC)]
    along_z = [[z * NYH * NC + r for z in range(NZ)] for r in range(NYH * NC)]
    chunk = lax.all_gather(in_basis, "wide", axis=0, tiled=True, axis_index_groups=along_yh)
    chunk, grads = lax.optimization_barrier((chunk, grads))
    copies = jnp.broadcast_to(chunk[None], (NZ, *chunk.shape))
    got = lax.all_to_all(copies, "wide", 0, 0, axis_index_groups=along_z)
    got, grads = lax.optimization_barrier((got, other_core(grads)))
    return got.reshape(-1, chunk.shape[1]), grads


def gather_packed(activations, picked):
    width = activations.shape[1]
    half = picked.shape[0] // 2
    rest = jnp.concatenate([picked[:half, width:], picked[half:, width:]], axis=1)
    packed = jnp.concatenate([activations, picked[:, :width], rest], axis=0)
    return lax.all_gather(packed, "narrow", axis=0, tiled=True)


def power_of(top):
    return jnp.maximum(jnp.floor(jnp.log2(jnp.maximum(top, 1e-30))), -100.0)


def pick(out_basis, core):
    width = out_basis.shape[1]
    own = width // (NZ * NYH * NC)
    source = lax.broadcasted_iota(jnp.int32, (width, width // NC), 0)
    place = lax.broadcasted_iota(jnp.int32, (width, width // NC), 1)
    wanted = ((place // own) * NC + core) * own + place % own
    return jnp.dot(out_basis, (source == wanted).astype(BF16), preferred_element_type=F32).astype(BF16)


def scatter_sum(total, top):
    blocks = NZ * NYH
    groups = [[zy * NC + c for zy in range(blocks)] for c in range(NC)]
    rows, columns = total.shape[0] // blocks, total.shape[1]
    tiles = (rows // 8, columns // 128)
    power = power_of(top)
    coded = (total * jnp.exp2(14.0 - power)).astype(F16)
    coded = coded.reshape(blocks, tiles[0], 8, tiles[1], 128).transpose(0, 1, 3, 2, 4).reshape(blocks, -1, 128)
    label = jnp.broadcast_to(power.astype(F16), (blocks, 8, 128))
    got = lax.all_to_all(
        jnp.concatenate([coded, label], axis=1), "wide", 0, 0, tiled=True, axis_index_groups=groups
    )
    scale = jnp.exp2(got[:, -8:-7, :1].astype(F32) - 14.0)
    summed = jnp.sum(got[:, :-8, :].astype(F32) * scale, axis=0)
    return summed.reshape(tiles[0], tiles[1], 8, 128).transpose(0, 2, 1, 3).reshape(rows, columns)


def shards(activations, out_grads, in_basis, out_basis, valid):
    wide, narrow = lax.axis_index("wide"), lax.axis_index("narrow")
    z, yh, core = wide // (NYH * NC), (wide // NC) % NYH, wide % NC
    yl, x = narrow // NX, narrow % NX
    pos = jnp.stack([z, yl, x, core]).astype(jnp.int32)
    sequences = activations.shape[0] // SEQ * lax.axis_size("wide")

    gathered = gather_packed(activations, pick(out_basis, core))
    mine, grads_other = gather_in_basis(in_basis, out_grads)
    other = other_core(mine)
    gathered, other = lax.optimization_barrier((gathered, other))
    mask = valid.astype(F32)[:, None]
    masked_in = rotate_in(pos, gathered, mine, other, mask)
    masked_other = other_core(masked_in)
    out_mine, out_theirs = rotate_out(gathered, out_grads, grads_other)
    total, top = squares(out_mine, out_theirs, masked_in, masked_other)
    return scatter_sum(total, jnp.max(top)) / sequences


def solution(mesh):
    in_specs = (
        P("wide", "narrow"),
        P("wide", None),
        P("wide", "narrow"),
        P("narrow", None),
        P("wide"),
    )
    out_specs = P("wide", "narrow")
    return jax.shard_map(shards, mesh=mesh, in_specs=in_specs, out_specs=out_specs, check_vma=False)
```
